32 devices in a mesh: row: 8 (over y, x, core), col: 4 (over z).
Axes of the slice: x: 2, y: 2, z: 4, core: 2. Of those that a mesh axis runs over, the one named last changes fastest.
Arguments:
- diag_inverse: float32 [512, 512], replicated, may hold values from -1 to 2, as said below
- panel: float32 [12288, 512], P('row', 'col'), may hold values from -0.3 to 0.3
- trailing: float32 [12288, 12288], P('row', 'col'), may hold values from -6 to 6
- agg_vals: float32 [8, 4, 12, 1024], P('row', 'col'), may hold values from -6 to 6
- agg_dest: int32 [8, 4, 12, 1], P('row', 'col'), may hold values from 0 to 7; in each aligned block of 12 rows (0 to 11, 12 to 23, ..., all dimensions but the last counted through in order) at most 2 rows name the same one
- agg_tile: int32 [8, 4, 12], P('row', 'col'), may hold values from 0 to 4607
Outputs:
- updated: float32 [12288, 12288], P('row', 'col')
- panel_factor: float32 [12288, 512], P('row', 'col')
The draws below stay inside these ranges and needn't reach their ends.
Inputs may be any that keep to these rules, and one draw needn't show every extreme that they name: `diag_inverse`: lower triangular with diagonal entries between 0.5 and 2. `agg_dest`: among the aggregates of one device no row index is named more than 2 times, and in some device one is named exactly 2 times.
All inputs are finite; a program needn't handle non-finite values.
Results may differ from the reference program's by a relative error of at most 0.000071.
Values sent between devices are 32-bit elements; how exact they have to be, the bound alone decides.
No kernel may reach another device: no remote copies, remote signals or barrier semaphores. Data moves between devices by JAX's collectives and lax.ppermute only.
A program may use at most 128 MiB of HBM per device.

```python
import math
import jax
import jax.numpy as jnp
import numpy as np
from jax import lax

B = 512
TRAIL = 12288
TILE_ROWS = 8
TILE_COLS = 128
CAP = 2
ROWS_DEV = 1536
COLS_DEV = 3072
TILES_DEV = 4608
AGG = 12
N_ROW = 8
N_COL = 4


def draw_diag_inverse(key, part):
    first_key, second_key = jax.random.split(key)
    diagonal_part = jax.random.uniform(first_key, (B,), jnp.float32, 0.6, 1.6)
    spread_part = jnp.clip(jax.random.normal(second_key, (B, B), jnp.float32), -4.0, 4.0) * (0.7 / math.sqrt(B))
    return jnp.tril(spread_part, -1) + jnp.diag(diagonal_part)


def touch_ends(array, key, smallest, high):
    shape = array.shape
    place = [jax.random.randint(jax.random.fold_in(key, axis), (), 0, shape[axis]) for axis in range(len(shape))]
    array = array.at[tuple(place)].set(smallest)
    longest = shape.index(max(shape))
    place[longest] = (place[longest] + 1) % shape[longest]
    return array.at[tuple(place)].set(high)


def levels(stream_key, dims, pieces, low, largest):
    def one(dim, parts):
        steps = jax.random.uniform(jax.random.fold_in(jax.random.fold_in(stream_key, 6), dim), (parts,), jnp.float32, low / len(pieces), largest / len(pieces))
        return jnp.repeat(jnp.exp(steps), dims[dim] // parts).reshape((-1,) + (1,) * (len(dims) - dim - 1))

    loudness = one(*pieces[0])
    for cut in pieces[1:]:
        loudness = loudness * one(*cut)
    return loudness


def shared_out(rng, own, number, rows, amount, top, bound, slope):
    order = jax.random.permutation(rng, amount)
    packed, usual = load_shares(amount, rows * top, bound, slope, True), load_shares(amount, rows * top, bound, slope, False)
    places = jnp.arange(amount)

    def named(tallies, offset_by):
        used = int((tallies > 0).sum())
        fixed = max(1, used // 4)
        shifted = fixed + (places - fixed + offset_by * (used - fixed)) % max(1, amount - fixed)
        return jnp.zeros((amount,), jnp.int32).at[order[jnp.where(places < fixed, places, shifted)]].set(jnp.asarray(tallies, jnp.int32))

    tallies = jnp.where(number % 4 == 0, named(packed, number // 4), named(usual, number - number // 4 - 1))
    mixed = jax.random.permutation(jax.random.fold_in(own, 3), amount)
    giver, receiver = mixed[0:amount // 2 * 2:2], mixed[1:amount // 2 * 2:2]
    margin = jnp.minimum(tallies[giver] - 1, bound - tallies[receiver]) // 2
    margin = jnp.where((giver == order[0]) | (receiver == order[0]) | (tallies[receiver] == 0), 0, jnp.maximum(margin, 0))
    shifted = jax.random.randint(jax.random.fold_in(own, 4), (amount // 2,), 0, 1 << 20) % (margin + 1)
    tallies = tallies.at[giver].add(-shifted).at[receiver].add(shifted)
    members = jnp.searchsorted(jnp.cumsum(tallies), jnp.arange(rows * top), side="right").astype(jnp.int32)
    grid = members.reshape(top, rows).T
    grid = grid[jax.random.permutation(jax.random.fold_in(own, 1), rows)]
    offset_by = jax.random.randint(jax.random.fold_in(own, 2), (rows, 1), 0, top)
    return jnp.take_along_axis(grid, (jnp.arange(top)[None, :] + offset_by) % top, axis=1)


def load_shares(count, total, reach, skew, full):
    portions = [(1 << 20) // math.isqrt(grade ** skew) + 1 for grade in range(1, count + 1)]
    largest = reach if full else min(reach, max(-(-total // count), total * portions[0] // sum(portions)))
    least = 1 if total - largest >= count - 1 else 0
    counts, surplus = [largest] + [least] * (count - 1), total - largest - least * (count - 1)
    while surplus > 0:
        free = [i for i in range(1, count) if counts[i] < largest] or [i for i in range(1, count) if counts[i] < reach]
        whole, left = sum([portions[i] for i in free]), surplus
        for i in free:
            more = min(reach - counts[i], max(1, left * portions[i] // whole), surplus)
            counts[i] = counts[i] + more
            surplus = surplus - more
    return np.array(counts)


def noise(key, dims, scale, bound, cuts=(), kind=jnp.bfloat16):
    drawn = jax.random.normal(key, dims, jnp.float32) * scale
    if len(cuts) > 0:
        drawn = levels(key, dims, cuts, -0.22, 0.18) * drawn
    return jnp.clip(drawn, min=-bound, max=bound).astype(kind)


def setup_inputs(seed: int = 0) -> dict:
    key_list = jax.random.split(jax.random.key(seed), 7)
    diag_inverse = draw_diag_inverse(jax.random.fold_in(key_list[6], 71), 0)
    panel = noise(key_list[1], (TRAIL, B), 0.05, 0.3, ((0, 8), (1, 4)), jnp.float32)
    trailing = noise(key_list[2], (TRAIL, TRAIL), 1.0, 6.0, ((0, 8), (1, 4)), jnp.float32)
    agg_vals = noise(key_list[3], (N_ROW, N_COL, AGG, TILE_ROWS * TILE_COLS), 1.0, 6.0, ((0, 8), (1, 4)), jnp.float32)
    agg_dest_keys = jax.random.split(jax.random.fold_in(key_list[4], 1), N_ROW * N_COL * AGG // AGG)
    agg_dest_turns = jax.random.permutation(jax.random.fold_in(key_list[4], 3), N_ROW * N_COL * AGG // AGG)
    agg_dest = jax.vmap(lambda own, number: shared_out(jax.random.fold_in(key_list[4], 2), own, number, AGG, N_ROW, 1, CAP, 1))(agg_dest_keys, agg_dest_turns).reshape((N_ROW, N_COL, AGG, 1))
    agg_tile = touch_ends(jax.random.randint(key_list[5], (N_ROW, N_COL, AGG), 0, TILES_DEV), jax.random.fold_in(key_list[5], 1), 0, TILES_DEV - 1).astype(jnp.int32)
    return dict(diag_inverse=diag_inverse, panel=panel, trailing=trailing, agg_vals=agg_vals, agg_dest=agg_dest, agg_tile=agg_tile)


def reference(diag_inverse, panel, trailing, agg_vals, agg_dest, agg_tile):
    panel_factor = jnp.dot(panel, diag_inverse.T, precision=lax.Precision.HIGHEST, preferred_element_type=jnp.float32)
    tile_rows = ROWS_DEV // TILE_ROWS
    tile_cols = COLS_DEV // TILE_COLS
    blocked = trailing.reshape(N_ROW, tile_rows, TILE_ROWS, N_COL, tile_cols, TILE_COLS)
    targets = agg_dest[..., 0].astype(jnp.int32)
    columns = jnp.broadcast_to(jnp.arange(N_COL, dtype=jnp.int32)[None, :, None], targets.shape)
    tile_row_ids = (agg_tile // tile_cols).astype(jnp.int32)
    tile_col_ids = (agg_tile % tile_cols).astype(jnp.int32)
    tiles_in = agg_vals.reshape(N_ROW, N_COL, AGG, TILE_ROWS, TILE_COLS)
    blocked = blocked.at[targets, tile_row_ids, :, columns, tile_col_ids, :].add(tiles_in)
    assembled = blocked.reshape(TRAIL, TRAIL)
    product = jnp.dot(panel_factor, panel_factor.T, precision=lax.Precision.HIGHEST, preferred_element_type=jnp.float32)
    updated = assembled - product
    return updated, panel_factor
```

```python
import functools

import jax
import jax.numpy as jnp
from jax import lax
from jax.experimental import pallas as pl
from jax.experimental.pallas import tpu as pltpu
from jax.sharding import PartitionSpec as P

TILE_ROWS = 8
TILE_COLS = 128
CAP = 2
NEXT = {0: 1, 1: 3, 3: 2, 2: 0}
PREV = {v: k for k, v in NEXT.items()}
BOTH = ("row", "col")
SMALL_GATHER = 4 << 20
NN = (((1,), (0,)), ((), ()))
NT = (((1,), (1,)), ((), ()))


def split(x):
    hi = x.astype(jnp.bfloat16)
    lo = (x - hi.astype(jnp.float32)).astype(jnp.bfloat16)
    return hi, lo


def hop(x, source, target, row_devices, col_devices):
    perm = [
        (((q ^ source) * 2 + k) * col_devices + q, ((q ^ target) * 2 + k) * col_devices + q)
        for q in range(col_devices)
        for k in range(2)
    ]
    return lax.ppermute(x, BOTH, perm)


def pick_kernel(role_ref, *refs):
    choices, out_ref, sem = refs[:-2], refs[-2], refs[-1]
    half = out_ref.shape[0] // 2
    role = role_ref[0]
    first, second = choices[:4], choices[4:]
    for r in range(4):

        @pl.when(role == r)
        def _(r=r):
            one = pltpu.make_async_copy(first[r], out_ref.at[pl.ds(0, half)], sem.at[0])
            two = pltpu.make_async_copy(second[r], out_ref.at[pl.ds(half, half)], sem.at[1])
            one.start()
            two.start()
            one.wait()
            two.wait()


def pick(role, first, second):
    rows, width = first[0].shape
    return pl.pallas_call(
        pick_kernel,
        out_shape=jax.ShapeDtypeStruct((2 * rows, width), jnp.float32),
        in_specs=[pl.BlockSpec(memory_space=pltpu.SMEM)]
        + [pl.BlockSpec(memory_space=pl.ANY)] * 8,
        out_specs=pl.BlockSpec(memory_space=pl.ANY),
        scratch_shapes=[pltpu.SemaphoreType.DMA((2,))],
        name="pick",
    )(role, *first, *second)


def front_kernel(
    own_plan,
    pair_plan,
    bm,
    bn,
    place_ref,
    entry_ref,
    start_ref,
    d_ref,
    dt_ref,
    agg_ref,
    trail_ref,
    *refs,
):
    n_own, n_pair = len(own_plan), len(pair_plan)
    own_refs = refs[:n_own]
    pair_refs = refs[n_own : n_own + n_pair]
    out_ref, block_ref = refs[n_own + n_pair : n_own + n_pair + 2]
    own_stage, pair_stage, dcat, dtcat, own_cat, pair_cat, own_full, sem = refs[
        n_own + n_pair + 2 :
    ]
    i, j = pl.program_id(0), pl.program_id(1)
    n_j = pl.num_programs(1)
    width = d_ref.shape[0]
    part = own_stage.shape[1] // 4

    def lanes(s):
        return pl.ds(pl.multiple_of(place_ref[s] * part, part), part)

    def copies():
        out = []
        for n, (s, base, row, rows) in enumerate(pair_plan):
            at = pl.multiple_of(place_ref[4 + base] + row, 16)
            out.append(
                pltpu.make_async_copy(
                    pair_refs[n], pair_stage.at[pl.ds(at, rows), lanes(s)], sem.at[n]
                )
            )
        for n, (s, row, rows) in enumerate(own_plan):
            out.append(
                pltpu.make_async_copy(
                    own_refs[n], own_stage.at[pl.ds(row, rows), lanes(s)], sem.at[n_pair + n]
                )
            )
        return out

    @pl.when((i == 0) & (j == 0))
    def _():
        todo = copies()
        for c in todo:
            c.start()
        hi, lo = split(d_ref[...])
        dcat[:, 0:width] = hi
        dcat[:, width : 2 * width] = hi
        dcat[:, 2 * width :] = lo
        hi, lo = split(dt_ref[...])
        dtcat[0:width, :] = hi
        dtcat[width : 2 * width, :] = hi
        dtcat[2 * width :, :] = lo
        for c in todo:
            c.wait()

        def body(n, carry):
            at = pl.ds(pl.multiple_of(n * width, width), width)
            hi, lo = split(pair_stage[at, :])
            rhs = jnp.concatenate([hi, lo, hi], axis=1)
            turned = lax.dot_general(dcat[...], rhs, NT, preferred_element_type=jnp.float32)
            hi, lo = split(turned)
            pair_cat[0:width, at] = hi
            pair_cat[width : 2 * width, at] = lo
            pair_cat[2 * width :, at] = hi
            return carry

        lax.fori_loop(0, pair_stage.shape[0] // width, body, 0)

    @pl.when(j == 0)
    def _():
        hi, lo = split(own_stage[pl.ds(pl.multiple_of(i * bm, bm), bm), :])
        lhs = jnp.concatenate([hi, lo, hi], axis=1)
        full = lax.dot_general(lhs, dtcat[...], NN, preferred_element_type=jnp.float32)
        own_full[...] = full
        block_ref[...] = own_full[:, pl.ds(pl.multiple_of(place_ref[6] * part, part), part)]
        hi, lo = split(full)
        own_cat[:, 0:width] = hi
        own_cat[:, width : 2 * width] = hi
        own_cat[:, 2 * width :] = lo

    cols = pl.ds(pl.multiple_of(j * bn, bn), bn)
    product = lax.dot_general(
        own_cat[...], pair_cat[:, cols], NN, preferred_element_type=jnp.float32
    )
    out_ref[...] = trail_ref[...] - product
    step = i * n_j + j

    def add(e, carry):
        r = pl.multiple_of(entry_ref[1, e], TILE_ROWS)
        c = pl.multiple_of(entry_ref[2, e], TILE_COLS)
        here = (pl.ds(r, TILE_ROWS), pl.ds(c, TILE_COLS))
        out_ref[here] = out_ref[here] + agg_ref[entry_ref[0, e]]
        return carry

    lax.fori_loop(start_ref[step], start_ref[step + 1], add, 0)


def front(place, entries, starts, d, agg, trailing, own, own_plan, pair, pair_plan, bm, bn):
    rows, cols = trailing.shape
    width = d.shape[0]
    part = width // 4
    anywhere = pl.BlockSpec(memory_space=pl.ANY)
    whole = pl.BlockSpec(memory_space=pltpu.VMEM)
    smem = pl.BlockSpec(memory_space=pltpu.SMEM)
    return pl.pallas_call(
        functools.partial(front_kernel, own_plan, pair_plan, bm, bn),
        grid=(rows // bm, cols // bn),
        out_shape=(
            jax.ShapeDtypeStruct((rows, cols), jnp.float32),
            jax.ShapeDtypeStruct((rows, part), jnp.float32),
        ),
        in_specs=[smem, smem, smem, whole, whole, whole]
        + [pl.BlockSpec((bm, bn), lambda i, j: (i, j))]
        + [anywhere] * (len(own) + len(pair)),
        out_specs=(
            pl.BlockSpec((bm, bn), lambda i, j: (i, j)),
            pl.BlockSpec((bm, part), lambda i, j: (i, 0)),
        ),
        scratch_shapes=[
            pltpu.VMEM((rows, width), jnp.float32),
            pltpu.VMEM((cols, width), jnp.float32),
            pltpu.VMEM((width, 3 * width), jnp.bfloat16),
            pltpu.VMEM((3 * width, width), jnp.bfloat16),
            pltpu.VMEM((bm, 3 * width), jnp.bfloat16),
            pltpu.VMEM((3 * width, cols), jnp.bfloat16),
            pltpu.VMEM((bm, width), jnp.float32),
            pltpu.SemaphoreType.DMA((len(own) + len(pair),)),
        ],
        compiler_params=pltpu.CompilerParams(vmem_limit_bytes=56 << 20),
        name="front",
    )(place, entries, starts, d, d.T, agg, trailing, *own, *pair)


def exchange_tiles(agg_vals, agg_dest, agg_tile, tiles_dev):
    row_devices = lax.axis_size("row")
    agg = agg_vals.shape[2]
    values = agg_vals.reshape(agg, TILE_ROWS, TILE_COLS)
    targets = agg_dest.reshape(-1)
    tile_ids = agg_tile.reshape(-1)
    if row_devices * agg * TILE_ROWS * TILE_COLS * 4 <= SMALL_GATHER:
        numbers = jnp.stack([targets, tile_ids]).astype(jnp.float32)
        numbers = jnp.pad(numbers, ((0, TILE_ROWS - 2), (0, TILE_COLS - agg)))
        got = lax.all_gather(jnp.concatenate([values, numbers[None]]), "row", axis=0)
        dest = got[:, agg, 0, :agg].astype(jnp.int32)
        ids = got[:, agg, 1, :agg].astype(jnp.int32)
        landing = jnp.where(dest == lax.axis_index("row"), ids, tiles_dev)
        landing = jnp.pad(landing, ((0, 0), (0, 1)), constant_values=tiles_dev)
        return got.reshape(-1, TILE_ROWS, TILE_COLS), landing.reshape(-1)
    matches = (targets[:, None] == jnp.arange(row_devices, dtype=jnp.int32)[None, :]).astype(
        jnp.int32
    )
    earlier = jnp.cumsum(matches, axis=0) - matches
    position = targets * CAP + jnp.sum(earlier * matches, axis=1)
    slots = row_devices * CAP
    send_values = jnp.zeros((slots, TILE_ROWS, TILE_COLS), jnp.float32).at[position].set(values)
    send_ids = jnp.full((slots,), tiles_dev, jnp.int32).at[position].set(tile_ids)
    got = lax.all_to_all(send_values, "row", split_axis=0, concat_axis=0, tiled=True)
    ids = lax.all_to_all(send_ids, "row", split_axis=0, concat_axis=0, tiled=True)
    return got, ids


def order_tiles(landing, slots, tiles_dev, tile_cols, bm, bn, n_i, n_j):
    row = (landing // tile_cols) * TILE_ROWS
    col = (landing % tile_cols) * TILE_COLS
    count = landing.shape[0]
    number = jnp.arange(count, dtype=jnp.int32)
    step = jnp.where(landing < tiles_dev, (row // bm) * n_j + col // bn, n_i * n_j)
    key = step * count + number
    rank = jnp.sum((key[None, :] < key[:, None]).astype(jnp.int32), axis=1)
    hit = (rank[None, :] == jnp.arange(slots, dtype=jnp.int32)[:, None]).astype(jnp.int32)
    fields = jnp.stack([number, row % bm, col % bn])
    entries = jnp.sum(hit[None] * fields[:, None, :], axis=2)
    edges = jnp.arange(n_i * n_j + 1, dtype=jnp.int32)
    starts = jnp.sum((step[None, :] < edges[:, None]).astype(jnp.int32), axis=1)
    return entries, starts


def per_device(diag_inverse, panel, trailing, agg_vals, agg_dest, agg_tile):
    row_devices = lax.axis_size("row")
    col_devices = lax.axis_size("col")
    local_rows, local_cols = trailing.shape
    col_index = lax.axis_index("col")
    row_index = lax.axis_index("row")
    tile_cols = local_cols // TILE_COLS
    tiles_dev = (local_rows // TILE_ROWS) * tile_cols
    bm = 512 if local_rows % 512 == 0 else local_rows
    bn = 768
    n_i, n_j = local_rows // bm, local_cols // bn

    agg, landing = exchange_tiles(agg_vals, agg_dest, agg_tile, tiles_dev)

    if row_devices == 8 and col_devices == 4:
        half = local_rows // 2
        role = (row_index // 2) ^ col_index
        core = row_index % 2
        siblings = [(p, p ^ 1) for p in range(row_devices)]
        ring = list(NEXT.items())
        parts = [(panel[:half], panel[half:])]
        for _ in range(3):
            parts.append(tuple(lax.ppermute(x, "col", ring) for x in parts[-1]))
        mine, other = [], []
        move = functools.partial(hop, row_devices=row_devices, col_devices=col_devices)
        for first, second in parts:
            a1 = move(first, 0, 1)
            b1 = move(second, 0, 2)
            a2 = move(a1, 1, 3)
            b2 = move(b1, 2, 3)
            a3 = move(a2, 3, 2)
            b3 = move(b2, 3, 1)
            got = pick(role.reshape(1), (first, a1, a3, a2), (second, b3, b1, b2))
            mine.append(got)
            other.append(lax.ppermute(got, "row", siblings))
        sources = [jnp.arange(4, dtype=jnp.int32)]
        back = jnp.array([PREV[q] for q in range(4)], jnp.int32)
        for _ in range(3):
            sources.append(back[sources[-1]])
        order = jnp.stack(sources)[:, col_index]
        place = jnp.concatenate(
            [order, jnp.stack([core * local_rows, (1 - core) * local_rows, col_index])]
        ).astype(jnp.int32)
        own = [x for pieces in parts for x in pieces]
        own_plan = [(s, r * half, half) for s in range(4) for r in range(2)]
        pair = mine + other
        pair_plan = [(s, b, 0, local_rows) for b in range(2) for s in range(4)]
    else:
        whole = lax.all_gather(panel, "col", axis=0)
        column = lax.all_gather(panel, "row", axis=0, tiled=True)
        column = column.reshape(col_devices, local_cols, panel.shape[1])
        partner = lax.all_to_all(column, "col", split_axis=0, concat_axis=0, tiled=True)
        own = [whole[s] for s in range(col_devices)]
        own_plan = [(s, 0, local_rows) for s in range(col_devices)]
        pair = [partner[s] for s in range(col_devices)]
        pair_plan = [(s, 0, 0, local_cols) for s in range(col_devices)]
        place = jnp.concatenate(
            [jnp.arange(4), jnp.zeros(2, jnp.int32), col_index.reshape(1)]
        ).astype(jnp.int32)

    entries, starts = order_tiles(
        landing, row_devices * CAP, tiles_dev, tile_cols, bm, bn, n_i, n_j
    )
    return front(
        place,
        entries,
        starts,
        diag_inverse,
        agg,
        trailing,
        own,
        own_plan,
        pair,
        pair_plan,
        bm,
        bn,
    )


def solution(mesh):
    in_specs = (
        P(),
        P("row", "col"),
        P("row", "col"),
        P("row", "col", None, None),
        P("row", "col", None, None),
        P("row", "col", None),
    )
    out_specs = (P("row", "col"), P("row", "col"))
    return jax.shard_map(
        per_device, mesh=mesh, in_specs=in_specs, out_specs=out_specs, check_vma=False
    )
```

```python
import functools

import jax
import jax.numpy as jnp
from jax import lax
from jax.experimental import pallas as pl
from jax.experimental.pallas import tpu as pltpu
from jax.sharding import PartitionSpec as P

TILE_ROWS = 8
TILE_COLS = 128
CAP = 2
NEXT = {0: 1, 1: 3, 3: 2, 2: 0}
PREV = {v: k for k, v in NEXT.items()}
NN = (((1,), (0,)), ((), ()))
NT = (((1,), (1,)), ((), ()))


def split(x):
    hi = x.astype(jnp.bfloat16)
    lo = (x - hi.astype(jnp.float32)).astype(jnp.bfloat16)
    return hi, lo


def own_kernel(plan, rows_step, place_ref, d_ref, *refs):
    pieces = refs[: len(plan)]
    halves_ref, block_ref, stage, dtcat, full_ref, sem = refs[len(plan) :]
    width = d_ref.shape[0]
    part = stage.shape[1] // 4
    todo = []
    for n, (s, row, rows) in enumerate(plan):
        lanes = pl.ds(pl.multiple_of(place_ref[s] * part, part), part)
        todo.append(
            pltpu.make_async_copy(pieces[n], stage.at[pl.ds(row, rows), lanes], sem.at[n])
        )
    for c in todo:
        c.start()
    hi, lo = split(d_ref[...].T)
    dtcat[0:width, :] = hi
    dtcat[width : 2 * width, :] = hi
    dtcat[2 * width :, :] = lo
    for c in todo:
        c.wait()
    mine = pl.ds(pl.multiple_of(place_ref[4] * part, part), part)

    def body(n, carry):
        at = pl.ds(pl.multiple_of(n * rows_step, rows_step), rows_step)
        hi, lo = split(stage[at, :])
        lhs = jnp.concatenate([hi, lo, hi], axis=1)
        full = lax.dot_general(lhs, dtcat[...], NN, preferred_element_type=jnp.float32)
        full_ref[...] = full
        block_ref[at, :] = full_ref[:, mine]
        hi, lo = split(full)
        halves_ref[at, 0:width] = hi
        halves_ref[at, width:] = lo
        return carry

    lax.fori_loop(0, stage.shape[0] // rows_step, body, 0)


def own_factor(place, d, pieces, plan, rows, rows_step):
    width = d.shape[0]
    part = width // 4
    whole = pl.BlockSpec(memory_space=pltpu.VMEM)
    return pl.pallas_call(
        functools.partial(own_kernel, plan, rows_step),
        out_shape=(
            jax.ShapeDtypeStruct((rows, 2 * width), jnp.bfloat16),
            jax.ShapeDtypeStruct((rows, part), jnp.float32),
        ),
        in_specs=[pl.BlockSpec(memory_space=pltpu.SMEM), whole]
        + [pl.BlockSpec(memory_space=pl.ANY)] * len(pieces),
        out_specs=(whole, whole),
        scratch_shapes=[
            pltpu.VMEM((rows, width), jnp.float32),
            pltpu.VMEM((3 * width, width), jnp.bfloat16),
            pltpu.VMEM((rows_step, width), jnp.float32),
            pltpu.SemaphoreType.DMA((len(pieces),)),
        ],
        compiler_params=pltpu.CompilerParams(vmem_limit_bytes=40 << 20),
        cost_estimate=pl.CostEstimate(
            flops=6 * rows * width * width, bytes_accessed=10 * rows * width, transcendentals=0
        ),
        name="own_factor",
    )(place, d, *pieces)


def front_kernel(
    first, entry_ref, start_ref, d_ref, agg_ref, pair_ref, own_ref, trail_ref, *refs
):
    out_ref, dcat, pair_cat = refs[-3:]
    j, i = pl.program_id(0), pl.program_id(1)
    n_i = pl.num_programs(1)
    bm, bn = out_ref.shape
    width = d_ref.shape[0]
    part = width // 4

    @pl.when((i == 0) & (j == 0))
    def _():
        hi, lo = split(d_ref[...])
        dcat[:, 0:width] = hi
        dcat[:, width : 2 * width] = hi
        dcat[:, 2 * width :] = lo

    @pl.when(i == 0)
    def _():
        panel = jnp.concatenate([pair_ref[:, s].reshape(bn, part) for s in range(4)], axis=1)
        hi, lo = split(panel)
        rhs = jnp.concatenate([hi, lo, hi], axis=1)
        turned = lax.dot_general(dcat[...], rhs, NT, preferred_element_type=jnp.float32)
        hi, lo = split(turned)
        pair_cat[0:width, :] = hi
        pair_cat[width : 2 * width, :] = lo
        pair_cat[2 * width :, :] = hi

    rows = pl.ds(pl.multiple_of(i * bm, bm), bm)
    hi, lo = own_ref[rows, 0:width], own_ref[rows, width:]
    lhs = jnp.concatenate([hi, hi, lo], axis=1)
    product = lax.dot_general(lhs, pair_cat[...], NN, preferred_element_type=jnp.float32)
    out_ref[...] = trail_ref[...] - product
    step = (first + j) * n_i + i

    def add(e, carry):
        r = pl.multiple_of(entry_ref[1, e], TILE_ROWS)
        c = pl.multiple_of(entry_ref[2, e], TILE_COLS)
        here = (pl.ds(r, TILE_ROWS), pl.ds(c, TILE_COLS))
        out_ref[here] = out_ref[here] + agg_ref[entry_ref[0, e]]
        return carry

    lax.fori_loop(start_ref[step], start_ref[step + 1], add, 0)


def front(entries, starts, d, agg, pair, own, trailing, before, first, n_j, bm, bn):
    rows, cols = trailing.shape
    width = d.shape[0]
    part = width // 4
    piece = pair.shape[2]
    if piece < bn:
        pair_block = pl.BlockSpec((bn // piece, 4, piece, part), lambda j, i: (j, 0, 0, 0))
    else:
        pair_block = pl.BlockSpec((1, 4, bn, part), lambda j, i: (0, 0, j, 0))
    whole = pl.BlockSpec(memory_space=pltpu.VMEM)
    smem = pl.BlockSpec(memory_space=pltpu.SMEM)
    block = pl.BlockSpec((bm, bn), lambda j, i: (i, first + j))
    operands = [entries, starts, d, agg, pair, own, trailing]
    specs = [smem, smem, whole, whole, pair_block, whole, block]
    aliases = {}
    if before is not None:
        aliases = {len(operands): 0}
        operands.append(before)
        specs.append(pl.BlockSpec(memory_space=pl.ANY))
    done = n_j * bn
    return pl.pallas_call(
        functools.partial(front_kernel, first),
        grid=(n_j, rows // bm),
        out_shape=jax.ShapeDtypeStruct((rows, cols), jnp.float32),
        in_specs=specs,
        out_specs=block,
        scratch_shapes=[
            pltpu.VMEM((width, 3 * width), jnp.bfloat16),
            pltpu.VMEM((3 * width, bn), jnp.bfloat16),
        ],
        input_output_aliases=aliases,
        compiler_params=pltpu.CompilerParams(vmem_limit_bytes=44 << 20),
        cost_estimate=pl.CostEstimate(
            flops=6 * (rows + width) * width * done,
            bytes_accessed=8 * rows * done + 4 * width * done,
            transcendentals=0,
        ),
        name="front",
    )(*operands)


def exchange_tiles(agg_vals, agg_dest, agg_tile, tiles_dev):
    row_devices = lax.axis_size("row")
    agg = agg_vals.shape[2]
    targets = agg_dest.reshape(-1)
    tile_ids = agg_tile.reshape(-1)
    slots = row_devices * CAP
    order = jnp.arange(agg, dtype=jnp.int32)
    earlier = (targets[None, :] == targets[:, None]) & (order[None, :] < order[:, None])
    position = targets * CAP + jnp.sum(earlier.astype(jnp.int32), axis=1)
    hit = position[None, :] == jnp.arange(slots, dtype=jnp.int32)[:, None]
    send_ids = tiles_dev + jnp.sum(jnp.where(hit, tile_ids[None, :] - tiles_dev, 0), axis=1)
    values = agg_vals.reshape(agg, TILE_ROWS, TILE_COLS)
    send = jnp.zeros((slots, TILE_ROWS, TILE_COLS), jnp.float32).at[position].set(values)
    send = send.reshape(row_devices, CAP, TILE_ROWS, TILE_COLS)
    numbers = send_ids.astype(jnp.float32).reshape(row_devices, 1, 1, CAP)
    numbers = jnp.pad(numbers, ((0, 0), (0, 0), (0, TILE_ROWS - 1), (0, TILE_COLS - CAP)))
    got = lax.all_to_all(
        jnp.concatenate([send, numbers], axis=1), "row", split_axis=0, concat_axis=0, tiled=True
    )
    landing = got[:, CAP, 0, :CAP].astype(jnp.int32)
    landing = jnp.pad(landing, ((0, 0), (0, 1)), constant_values=tiles_dev)
    return got.reshape(-1, TILE_ROWS, TILE_COLS), landing.reshape(-1)


def order_tiles(landing, slots, tiles_dev, tile_cols, bm, bn, n_i, n_j):
    row = (landing // tile_cols) * TILE_ROWS
    col = (landing % tile_cols) * TILE_COLS
    count = landing.shape[0]
    number = jnp.arange(count, dtype=jnp.int32)
    step = jnp.where(landing < tiles_dev, (col // bn) * n_i + row // bm, n_i * n_j)
    key = step * count + number
    rank = jnp.sum((key[None, :] < key[:, None]).astype(jnp.int32), axis=1)
    hit = (rank[None, :] == jnp.arange(slots, dtype=jnp.int32)[:, None]).astype(jnp.int32)
    fields = jnp.stack([number, row % bm, col % bn])
    entries = jnp.sum(hit[None] * fields[:, None, :], axis=2)
    edges = jnp.arange(n_i * n_j + 1, dtype=jnp.int32)
    starts = jnp.sum((step[None, :] < edges[:, None]).astype(jnp.int32), axis=1)
    return entries, starts


def per_device(diag_inverse, panel, trailing, agg_vals, agg_dest, agg_tile):
    row_devices = lax.axis_size("row")
    col_devices = lax.axis_size("col")
    local_rows, local_cols = trailing.shape
    part = panel.shape[1]
    col_index = lax.axis_index("col")
    tile_cols = local_cols // TILE_COLS
    tiles_dev = (local_rows // TILE_ROWS) * tile_cols
    bm = 512 if local_rows % 512 == 0 else local_rows
    bn = 768
    n_i, n_j = local_rows // bm, local_cols // bn

    if row_devices == 2 * col_devices and local_rows % (16 * row_devices) == 0:
        eighth = local_rows // row_devices
        spread = lax.all_to_all(
            panel.reshape(row_devices, eighth, part),
            "row",
            split_axis=0,
            concat_axis=0,
            tiled=True,
        )
        wanted = lax.all_to_all(
            spread.reshape(col_devices, 2, eighth, part),
            "col",
            split_axis=0,
            concat_axis=0,
            tiled=True,
        )
        pairs = [lax.all_gather(wanted[:, k], "row", axis=0) for k in range(2)]
        half = local_rows // 2
        ring = list(NEXT.items())
        parts = [(panel[:half], panel[half:])]
        for _ in range(3):
            parts.append(tuple(lax.ppermute(x, "col", ring) for x in parts[-1]))
        sources = [jnp.arange(4, dtype=jnp.int32)]
        back = jnp.array([PREV[q] for q in range(4)], jnp.int32)
        for _ in range(3):
            sources.append(back[sources[-1]])
        order = jnp.stack(sources)[:, col_index]
        own = [panel] + [x for pieces in parts[1:] for x in pieces]
        own_plan = [(0, 0, local_rows)]
        own_plan += [(s, r * half, half) for s in range(1, 4) for r in range(2)]
    else:
        whole = lax.all_gather(panel, "col", axis=0)
        column = lax.all_gather(panel, "row", axis=0, tiled=True)
        column = column.reshape(col_devices, local_cols, part)
        partner = lax.all_to_all(column, "col", split_axis=0, concat_axis=0, tiled=True)
        pairs = [partner[None]]
        own = [whole[s] for s in range(col_devices)]
        own_plan = [(s, 0, local_rows) for s in range(col_devices)]
        order = jnp.arange(4, dtype=jnp.int32)

    agg, landing = exchange_tiles(agg_vals, agg_dest, agg_tile, tiles_dev)
    entries, starts = order_tiles(
        landing, row_devices * CAP, tiles_dev, tile_cols, bm, bn, n_i, n_j
    )
    place = jnp.concatenate([order, col_index.reshape(1)]).astype(jnp.int32)
    halves, own_block = own_factor(place, diag_inverse, own, own_plan, local_rows, bm)
    updated = None
    calls = len(pairs)
    for h, pair in enumerate(pairs):
        updated = front(
            entries,
            starts,
            diag_inverse,
            agg,
            pair,
            halves,
            trailing,
            updated,
            h * (n_j // calls),
            n_j // calls,
            bm,
            bn,
        )
    return updated, own_block


def solution(mesh):
    in_specs = (
        P(),
        P("row", "col"),
        P("row", "col"),
        P("row", "col", None, None),
        P("row", "col", None, None),
        P("row", "col", None),
    )
    out_specs = (P("row", "col"), P("row", "col"))
    return jax.shard_map(
        per_device, mesh=mesh, in_specs=in_specs, out_specs=out_specs, check_vma=False
    )
```

```python
import functools

import jax
import jax.numpy as jnp
from jax import lax
from jax.experimental import pallas as pl
from jax.experimental.pallas import tpu as pltpu
from jax.sharding import PartitionSpec as P

TILE_ROWS = 8
TILE_COLS = 128
CAP = 2
VMEM_LIMIT = 58 << 20
NEXT = {0: 1, 1: 3, 3: 2, 2: 0}
PREV = {v: k for k, v in NEXT.items()}
NN = (((1,), (0,)), ((), ()))


def split(x):
    hi = x.astype(jnp.bfloat16)
    lo = (x - hi.astype(jnp.float32)).astype(jnp.bfloat16)
    return hi, lo


def own_kernel(plan, rows_step, place_ref, d_ref, *refs):
    pieces = refs[: len(plan)]
    halves_ref, block_ref, stage, dtcat, full_ref, sem = refs[len(plan) :]
    width = d_ref.shape[0]
    part = stage.shape[1] // 4
    todo = []
    for n, (s, row, rows) in enumerate(plan):
        lanes = pl.ds(pl.multiple_of(place_ref[s] * part, part), part)
        todo.append(
            pltpu.make_async_copy(pieces[n], stage.at[pl.ds(row, rows), lanes], sem.at[n])
        )
    for c in todo:
        c.start()
    hi, lo = split(d_ref[...].T)
    dtcat[0:width, :] = hi
    dtcat[width : 2 * width, :] = hi
    dtcat[2 * width :, :] = lo
    for c in todo:
        c.wait()
    mine = pl.ds(pl.multiple_of(place_ref[4] * part, part), part)

    def body(n, carry):
        at = pl.ds(pl.multiple_of(n * rows_step, rows_step), rows_step)
        hi, lo = split(stage[at, :])
        lhs = jnp.concatenate([hi, lo, hi], axis=1)
        full = lax.dot_general(lhs, dtcat[...], NN, preferred_element_type=jnp.float32)
        full_ref[...] = full
        block_ref[at, :] = full_ref[:, mine]
        hi, lo = split(full)
        halves_ref[at, 0:width] = hi
        halves_ref[at, width:] = lo
        return carry

    lax.fori_loop(0, stage.shape[0] // rows_step, body, 0)


def own_factor(place, d, pieces, plan, rows, rows_step):
    width = d.shape[0]
    part = width // 4
    whole = pl.BlockSpec(memory_space=pltpu.VMEM)
    return pl.pallas_call(
        functools.partial(own_kernel, plan, rows_step),
        out_shape=(
            jax.ShapeDtypeStruct((rows, 2 * width), jnp.bfloat16),
            jax.ShapeDtypeStruct((rows, part), jnp.float32),
        ),
        in_specs=[pl.BlockSpec(memory_space=pltpu.SMEM), whole]
        + [pl.BlockSpec(memory_space=pl.ANY)] * len(pieces),
        out_specs=(whole, whole),
        scratch_shapes=[
            pltpu.VMEM((rows, width), jnp.float32),
            pltpu.VMEM((3 * width, width), jnp.bfloat16),
            pltpu.VMEM((rows_step, width), jnp.float32),
            pltpu.SemaphoreType.DMA((len(pieces),)),
        ],
        compiler_params=pltpu.CompilerParams(vmem_limit_bytes=VMEM_LIMIT),
        cost_estimate=pl.CostEstimate(
            flops=6 * rows * width * width, bytes_accessed=10 * rows * width, transcendentals=0
        ),
        name="own_factor",
    )(place, d, *pieces)


def front_kernel(
    plan, place_ref, entry_ref, start_ref, d_ref, agg_ref, own_ref, trail_ref, *refs
):
    pieces = refs[: len(plan)]
    out_ref, stage, dcat, pair_cat, sem = refs[len(plan) :]
    j, i = pl.program_id(0), pl.program_id(1)
    n_i = pl.num_programs(1)
    bm, bn = out_ref.shape
    width = d_ref.shape[0]

    @pl.when((i == 0) & (j == 0))
    def _():
        todo = []
        for n, (where, half) in enumerate(plan):
            _, depth, cols = pieces[n].shape
            at = pl.ds(pl.multiple_of(place_ref[where] * depth, 8), depth)
            todo.append(
                pltpu.make_async_copy(
                    pieces[n], stage.at[:, at, pl.ds(half * cols, cols)], sem.at[n]
                )
            )
        for c in todo:
            c.start()
        hi, lo = split(d_ref[...])
        dcat[:, 0:width] = hi
        dcat[:, width : 2 * width] = hi
        dcat[:, 2 * width :] = lo
        for c in todo:
            c.wait()

    @pl.when(i == 0)
    def _():
        cols = pl.ds(pl.multiple_of(j * bn, bn), bn)
        hi, lo = split(stage[:, :, cols].reshape(width, bn))
        rhs = jnp.concatenate([hi, lo, hi], axis=0)
        turned = lax.dot_general(dcat[...], rhs, NN, preferred_element_type=jnp.float32)
        hi, lo = split(turned)
        pair_cat[0:width, :] = hi
        pair_cat[width : 2 * width, :] = lo
        pair_cat[2 * width :, :] = hi

    rows = pl.ds(pl.multiple_of(i * bm, bm), bm)
    hi, lo = own_ref[rows, 0:width], own_ref[rows, width:]
    lhs = jnp.concatenate([hi, hi, lo], axis=1)
    product = lax.dot_general(lhs, pair_cat[...], NN, preferred_element_type=jnp.float32)
    out_ref[...] = trail_ref[...] - product
    step = j * n_i + i

    def add(e, carry):
        r = pl.multiple_of(entry_ref[1, e], TILE_ROWS)
        c = pl.multiple_of(entry_ref[2, e], TILE_COLS)
        here = (pl.ds(r, TILE_ROWS), pl.ds(c, TILE_COLS))
        out_ref[here] = out_ref[here] + agg_ref[entry_ref[0, e]]
        return carry

    lax.fori_loop(start_ref[step], start_ref[step + 1], add, 0)


def front(place, entries, starts, d, agg, own, trailing, pieces, plan, bm, bn):
    rows, cols = trailing.shape
    width = d.shape[0]
    whole = pl.BlockSpec(memory_space=pltpu.VMEM)
    smem = pl.BlockSpec(memory_space=pltpu.SMEM)
    block = pl.BlockSpec((bm, bn), lambda j, i: (i, j))
    return pl.pallas_call(
        functools.partial(front_kernel, plan),
        grid=(cols // bn, rows // bm),
        out_shape=jax.ShapeDtypeStruct((rows, cols), jnp.float32),
        in_specs=[smem, smem, smem, whole, whole, whole, block]
        + [pl.BlockSpec(memory_space=pl.ANY)] * len(pieces),
        out_specs=block,
        scratch_shapes=[
            pltpu.VMEM((4, width // 4, cols), jnp.float32),
            pltpu.VMEM((width, 3 * width), jnp.bfloat16),
            pltpu.VMEM((3 * width, bn), jnp.bfloat16),
            pltpu.SemaphoreType.DMA((len(pieces),)),
        ],
        compiler_params=pltpu.CompilerParams(vmem_limit_bytes=VMEM_LIMIT),
        cost_estimate=pl.CostEstimate(
            flops=6 * (rows + width) * width * cols,
            bytes_accessed=8 * rows * cols + 4 * width * cols,
            transcendentals=0,
        ),
        name="front",
    )(place, entries, starts, d, agg, own, trailing, *pieces)


def exchange_tiles(agg_vals, agg_dest, agg_tile, tiles_dev):
    row_devices = lax.axis_size("row")
    agg = agg_vals.shape[2]
    targets = agg_dest.reshape(-1)
    tile_ids = agg_tile.reshape(-1)
    slots = row_devices * CAP
    order = jnp.arange(agg, dtype=jnp.int32)
    earlier = (targets[None, :] == targets[:, None]) & (order[None, :] < order[:, None])
    position = targets * CAP + jnp.sum(earlier.astype(jnp.int32), axis=1)
    hit = position[None, :] == jnp.arange(slots, dtype=jnp.int32)[:, None]
    send_ids = tiles_dev + jnp.sum(jnp.where(hit, tile_ids[None, :] - tiles_dev, 0), axis=1)
    values = agg_vals.reshape(agg, TILE_ROWS, TILE_COLS)
    send = jnp.zeros((slots, TILE_ROWS, TILE_COLS), jnp.float32).at[position].set(values)
    send = send.reshape(row_devices, CAP, TILE_ROWS, TILE_COLS)
    numbers = send_ids.astype(jnp.float32).reshape(row_devices, 1, 1, CAP)
    numbers = jnp.pad(numbers, ((0, 0), (0, 0), (0, TILE_ROWS - 1), (0, TILE_COLS - CAP)))
    got = lax.all_to_all(
        jnp.concatenate([send, numbers], axis=1), "row", split_axis=0, concat_axis=0, tiled=True
    )
    landing = got[:, CAP, 0, :CAP].astype(jnp.int32)
    landing = jnp.pad(landing, ((0, 0), (0, 1)), constant_values=tiles_dev)
    return got.reshape(-1, TILE_ROWS, TILE_COLS), landing.reshape(-1)


def order_tiles(landing, slots, tiles_dev, tile_cols, bm, bn, n_i, n_j):
    row = (landing // tile_cols) * TILE_ROWS
    col = (landing % tile_cols) * TILE_COLS
    count = landing.shape[0]
    number = jnp.arange(count, dtype=jnp.int32)
    step = jnp.where(landing < tiles_dev, (col // bn) * n_i + row // bm, n_i * n_j)
    key = step * count + number
    rank = jnp.sum((key[None, :] < key[:, None]).astype(jnp.int32), axis=1)
    hit = (rank[None, :] == jnp.arange(slots, dtype=jnp.int32)[:, None]).astype(jnp.int32)
    fields = jnp.stack([number, row % bm, col % bn])
    entries = jnp.sum(hit[None] * fields[:, None, :], axis=2)
    edges = jnp.arange(n_i * n_j + 1, dtype=jnp.int32)
    starts = jnp.sum((step[None, :] < edges[:, None]).astype(jnp.int32), axis=1)
    return entries, starts


def per_device(diag_inverse, panel, trailing, agg_vals, agg_dest, agg_tile):
    row_devices = lax.axis_size("row")
    col_devices = lax.axis_size("col")
    local_rows, local_cols = trailing.shape
    part = panel.shape[1]
    col_index = lax.axis_index("col")
    tile_cols = local_cols // TILE_COLS
    tiles_dev = (local_rows // TILE_ROWS) * tile_cols
    bm = 512 if local_rows % 512 == 0 else local_rows
    bn = 768
    n_i, n_j = local_rows // bm, local_cols // bn

    if row_devices == 8 and col_devices == 4:
        row_index = lax.axis_index("row")
        chip, core = row_index // 2, row_index % 2
        half = local_rows // 2
        ring = list(NEXT.items())
        parts = [(panel[:half], panel[half:])]
        parts.append(tuple(lax.ppermute(x, "col", ring) for x in parts[-1]))
        depth = part // row_devices
        spread = lax.all_to_all(
            panel.T.reshape(row_devices, depth, local_rows),
            "row",
            split_axis=0,
            concat_axis=0,
            tiled=True,
        )
        spread, parts[1] = lax.optimization_barrier((spread, parts[1]))
        wanted = lax.all_to_all(
            spread.reshape(col_devices, 2, depth, local_rows),
            "col",
            split_axis=0,
            concat_axis=0,
            tiled=True,
        )
        wanted, parts[1], agg_vals, agg_dest, agg_tile = lax.optimization_barrier(
            (wanted, parts[1], agg_vals, agg_dest, agg_tile)
        )
        for _ in range(2):
            parts.append(tuple(lax.ppermute(x, "col", ring) for x in parts[-1]))
        siblings = [(p, p ^ 1) for p in range(row_devices)]
        following = jnp.array([NEXT[c] for c in range(4)], jnp.int32)
        previous = jnp.array([PREV[c] for c in range(4)], jnp.int32)
        places, pieces, plan = [], [], []
        for k, (step, back) in enumerate(((NEXT, previous), (PREV, following))):
            turn = [(2 * c + m, 2 * step[c] + m) for c in range(4) for m in range(2)]
            piece, source = wanted[:, k], chip
            for n in range(4):
                if n > 0:
                    piece, source = lax.ppermute(piece, "row", turn), back[source]
                plan += [(5 + len(places), k), (6 + len(places), k)]
                places += [2 * source + core, 2 * source + 1 - core]
                pieces += [piece, lax.ppermute(piece, "row", siblings)]
        sources = [jnp.arange(4, dtype=jnp.int32)]
        for _ in range(3):
            sources.append(previous[sources[-1]])
        order = jnp.stack(sources)[:, col_index]
        own = [panel] + [x for halves in parts[1:] for x in halves]
        own_plan = [(0, 0, local_rows)]
        own_plan += [(s, r * half, half) for s in range(1, 4) for r in range(2)]
    else:
        whole = lax.all_gather(panel, "col", axis=0)
        column = lax.all_gather(panel, "row", axis=0, tiled=True)
        column = column.reshape(col_devices, local_cols, part)
        partner = lax.all_to_all(column, "col", split_axis=0, concat_axis=0, tiled=True)
        places, pieces, plan = [jnp.int32(0)], [jnp.swapaxes(partner, 1, 2)], [(5, 0)]
        own = [whole[s] for s in range(col_devices)]
        own_plan = [(s, 0, local_rows) for s in range(col_devices)]
        order = jnp.arange(4, dtype=jnp.int32)

    agg, landing = exchange_tiles(agg_vals, agg_dest, agg_tile, tiles_dev)
    entries, starts = order_tiles(
        landing, row_devices * CAP, tiles_dev, tile_cols, bm, bn, n_i, n_j
    )
    place = jnp.concatenate([order, jnp.stack([col_index] + places)]).astype(jnp.int32)
    halves, own_block = own_factor(place, diag_inverse, own, own_plan, local_rows, bm)
    updated = front(
        place, entries, starts, diag_inverse, agg, halves, trailing, pieces, plan, bm, bn
    )
    return updated, own_block


def solution(mesh):
    in_specs = (
        P(),
        P("row", "col"),
        P("row", "col"),
        P("row", "col", None, None),
        P("row", "col", None, None),
        P("row", "col", None),
    )
    out_specs = (P("row", "col"), P("row", "col"))
    return jax.shard_map(
        per_device, mesh=mesh, in_specs=in_specs, out_specs=out_specs, check_vma=False
    )
```

```python
import functools

import jax
import jax.numpy as jnp
from jax import lax
from jax.experimental import pallas as pl
from jax.experimental.pallas import tpu as pltpu
from jax.sharding import PartitionSpec as P

TILE_ROWS = 8
TILE_COLS = 128
CAP = 2
VMEM_LIMIT = 58 << 20
NEXT = {0: 1, 1: 3, 3: 2, 2: 0}
PREV = {v: k for k, v in NEXT.items()}
NN = (((1,), (0,)), ((), ()))
NT = (((1,), (1,)), ((), ()))


def split(x):
    hi = x.astype(jnp.bfloat16)
    lo = (x - hi.astype(jnp.float32)).astype(jnp.bfloat16)
    return hi, lo


def ring_place(index, steps):
    at = (index ^ (index >> 1)) - steps & 3
    return at ^ (at >> 1)


def own_kernel(ringed, plan, rows_step, place_ref, d_ref, *refs):
    pieces = refs[: len(plan)]
    halves_ref, block_ref, stage, dtcat, full_ref, sem = refs[len(plan) :]
    width = d_ref.shape[0]
    part = stage.shape[1] // 4
    todo = []
    for n, (s, row, rows) in enumerate(plan):
        source = ring_place(place_ref[1], s) if ringed else s
        lanes = pl.ds(pl.multiple_of(source * part, part), part)
        todo.append(
            pltpu.make_async_copy(pieces[n], stage.at[pl.ds(row, rows), lanes], sem.at[n])
        )
    for c in todo:
        c.start()
    hi, lo = split(d_ref[...].T)
    dtcat[0:width, :] = hi
    dtcat[width : 2 * width, :] = hi
    dtcat[2 * width :, :] = lo
    for c in todo:
        c.wait()
    mine = pl.ds(pl.multiple_of(place_ref[1] * part, part), part)

    def body(n, carry):
        at = pl.ds(pl.multiple_of(n * rows_step, rows_step), rows_step)
        hi, lo = split(stage[at, :])
        lhs = jnp.concatenate([hi, lo, hi], axis=1)
        full = lax.dot_general(lhs, dtcat[...], NN, preferred_element_type=jnp.float32)
        full_ref[...] = full
        block_ref[at, :] = full_ref[:, mine]
        hi, lo = split(full)
        halves_ref[at, 0:width] = hi
        halves_ref[at, width:] = lo
        return carry

    lax.fori_loop(0, stage.shape[0] // rows_step, body, 0)


def own_factor(place, d, pieces, plan, ringed, rows, rows_step):
    width = d.shape[0]
    part = width // 4
    whole = pl.BlockSpec(memory_space=pltpu.VMEM)
    return pl.pallas_call(
        functools.partial(own_kernel, ringed, plan, rows_step),
        out_shape=(
            jax.ShapeDtypeStruct((rows, 2 * width), jnp.bfloat16),
            jax.ShapeDtypeStruct((rows, part), jnp.float32),
        ),
        in_specs=[pl.BlockSpec(memory_space=pltpu.SMEM), whole]
        + [pl.BlockSpec(memory_space=pl.ANY)] * len(pieces),
        out_specs=(whole, whole),
        scratch_shapes=[
            pltpu.VMEM((rows, width), jnp.float32),
            pltpu.VMEM((3 * width, width), jnp.bfloat16),
            pltpu.VMEM((rows_step, width), jnp.float32),
            pltpu.SemaphoreType.DMA((len(pieces),)),
        ],
        compiler_params=pltpu.CompilerParams(vmem_limit_bytes=VMEM_LIMIT),
        cost_estimate=pl.CostEstimate(
            flops=6 * rows * width * width, bytes_accessed=10 * rows * width, transcendentals=0
        ),
        name="own_factor",
    )(place, d, *pieces)


def pair_kernel(d_ref, panel_ref, top_ref, low_ref):
    width = d_ref.shape[0]
    half = width // 2
    d_hi, d_lo = split(d_ref[...])
    hi, lo = split(jnp.concatenate([panel_ref[s] for s in range(4)], axis=1))
    for ref, rows, upto in ((top_ref, slice(0, half), half), (low_ref, slice(half, width), width)):
        d_rows = d_hi[rows, :upto]
        lhs = jnp.concatenate([d_rows, d_rows, d_lo[rows, :upto]], axis=1)
        rhs = jnp.concatenate([hi[:, :upto], lo[:, :upto], hi[:, :upto]], axis=1)
        ref[...] = lax.dot_general(lhs, rhs, NT, preferred_element_type=jnp.float32)


def pair_factor(d, panel, rows_step):
    width = d.shape[0]
    parts, rows, part = panel.shape
    out = jax.ShapeDtypeStruct((width // 2, rows), jnp.float32)
    out_block = pl.BlockSpec((width // 2, rows_step), lambda n: (0, n))
    return pl.pallas_call(
        pair_kernel,
        grid=(rows // rows_step,),
        out_shape=(out, out),
        in_specs=[
            pl.BlockSpec((width, width), lambda n: (0, 0)),
            pl.BlockSpec((parts, rows_step, part), lambda n: (0, n, 0)),
        ],
        out_specs=(out_block, out_block),
        compiler_params=pltpu.CompilerParams(vmem_limit_bytes=32 << 20),
        cost_estimate=pl.CostEstimate(
            flops=6 * rows * width * width, bytes_accessed=8 * rows * width, transcendentals=0
        ),
        name="pair_factor",
    )(d, panel)


def front_kernel(
    ringed, plan, place_ref, entry_ref, start_ref, agg_ref, own_ref, trail_ref, *refs
):
    pieces = refs[: len(plan)]
    out_ref, stage, pair_cat, sem = refs[len(plan) :]
    j, i = pl.program_id(0), pl.program_id(1)
    n_i = pl.num_programs(1)
    bm, bn = out_ref.shape
    width = stage.shape[0]

    @pl.when((i == 0) & (j == 0))
    def _():
        todo = []
        for n, (half, steps, swap) in enumerate(plan):
            depth, cols = pieces[n].shape
            block = 0
            if ringed:
                chip = ring_place(place_ref[0] // 2, steps)
                block = (place_ref[0] % 2 ^ swap) * 4 + chip
            at = pl.ds(pl.multiple_of(block * cols, TILE_COLS), cols)
            rows = pl.ds(half * depth, depth)
            todo.append(pltpu.make_async_copy(pieces[n], stage.at[rows, at], sem.at[n]))
        for c in todo:
            c.start()
        for c in todo:
            c.wait()

    @pl.when(i == 0)
    def _():
        cols = pl.ds(pl.multiple_of(j * bn, bn), bn)
        hi, lo = split(stage[:, cols])
        pair_cat[0:width, :] = hi
        pair_cat[width : 2 * width, :] = lo
        pair_cat[2 * width :, :] = hi

    rows = pl.ds(pl.multiple_of(i * bm, bm), bm)
    hi, lo = own_ref[rows, 0:width], own_ref[rows, width:]
    lhs = jnp.concatenate([hi, hi, lo], axis=1)
    product = lax.dot_general(lhs, pair_cat[...], NN, preferred_element_type=jnp.float32)
    out_ref[...] = trail_ref[...] - product
    step = j * n_i + i

    def add(e, carry):
        r = pl.multiple_of(entry_ref[1, e], TILE_ROWS)
        c = pl.multiple_of(entry_ref[2, e], TILE_COLS)
        here = (pl.ds(r, TILE_ROWS), pl.ds(c, TILE_COLS))
        out_ref[here] = out_ref[here] + agg_ref[entry_ref[0, e]]
        return carry

    lax.fori_loop(start_ref[step], start_ref[step + 1], add, 0)


def front(place, entries, starts, agg, own, trailing, pieces, plan, ringed, bm, bn):
    rows, cols = trailing.shape
    width = own.shape[1] // 2
    whole = pl.BlockSpec(memory_space=pltpu.VMEM)
    smem = pl.BlockSpec(memory_space=pltpu.SMEM)
    block = pl.BlockSpec((bm, bn), lambda j, i: (i, j))
    return pl.pallas_call(
        functools.partial(front_kernel, ringed, plan),
        grid=(cols // bn, rows // bm),
        out_shape=jax.ShapeDtypeStruct((rows, cols), jnp.float32),
        in_specs=[smem, smem, smem, whole, whole, block]
        + [pl.BlockSpec(memory_space=pl.ANY)] * len(pieces),
        out_specs=block,
        scratch_shapes=[
            pltpu.VMEM((width, cols), jnp.float32),
            pltpu.VMEM((3 * width, bn), jnp.bfloat16),
            pltpu.SemaphoreType.DMA((len(pieces),)),
        ],
        compiler_params=pltpu.CompilerParams(vmem_limit_bytes=VMEM_LIMIT),
        cost_estimate=pl.CostEstimate(
            flops=6 * rows * width * cols,
            bytes_accessed=8 * rows * cols + 4 * width * cols,
            transcendentals=0,
        ),
        name="front",
    )(place, entries, starts, agg, own, trailing, *pieces)


def exchange_tiles(agg_vals, agg_dest, agg_tile, tiles_dev):
    row_devices = lax.axis_size("row")
    agg = agg_vals.shape[2]
    targets = agg_dest.reshape(-1)
    tile_ids = agg_tile.reshape(-1)
    slots = row_devices * CAP
    order = jnp.arange(agg, dtype=jnp.int32)
    earlier = (targets[None, :] == targets[:, None]) & (order[None, :] < order[:, None])
    position = targets * CAP + jnp.sum(earlier.astype(jnp.int32), axis=1)
    hit = position[None, :] == jnp.arange(slots, dtype=jnp.int32)[:, None]
    send_ids = tiles_dev + jnp.sum(jnp.where(hit, tile_ids[None, :] - tiles_dev, 0), axis=1)
    values = agg_vals.reshape(agg, TILE_ROWS, TILE_COLS)
    send = jnp.zeros((slots, TILE_ROWS, TILE_COLS), jnp.float32).at[position].set(values)
    send = send.reshape(row_devices, CAP, TILE_ROWS, TILE_COLS)
    numbers = send_ids.astype(jnp.float32).reshape(row_devices, 1, 1, CAP)
    numbers = jnp.pad(numbers, ((0, 0), (0, 0), (0, TILE_ROWS - 1), (0, TILE_COLS - CAP)))
    got = lax.all_to_all(
        jnp.concatenate([send, numbers], axis=1), "row", split_axis=0, concat_axis=0, tiled=True
    )
    landing = got[:, CAP, 0, :CAP].astype(jnp.int32)
    landing = jnp.pad(landing, ((0, 0), (0, 1)), constant_values=tiles_dev)
    return got.reshape(-1, TILE_ROWS, TILE_COLS), landing.reshape(-1)


def order_tiles(landing, slots, tiles_dev, tile_cols, bm, bn, n_i, n_j):
    row = (landing // tile_cols) * TILE_ROWS
    col = (landing % tile_cols) * TILE_COLS
    count = landing.shape[0]
    number = jnp.arange(count, dtype=jnp.int32)
    step = jnp.where(landing < tiles_dev, (col // bn) * n_i + row // bm, n_i * n_j)
    key = step * count + number
    rank = jnp.sum((key[None, :] < key[:, None]).astype(jnp.int32), axis=1)
    hit = (rank[None, :] == jnp.arange(slots, dtype=jnp.int32)[:, None]).astype(jnp.int32)
    fields = jnp.stack([number, row % bm, col % bn])
    entries = jnp.sum(hit[None] * fields[:, None, :], axis=2)
    edges = jnp.arange(n_i * n_j + 1, dtype=jnp.int32)
    starts = jnp.sum((step[None, :] < edges[:, None]).astype(jnp.int32), axis=1)
    return entries, starts


def per_device(diag_inverse, panel, trailing, agg_vals, agg_dest, agg_tile):
    row_devices = lax.axis_size("row")
    col_devices = lax.axis_size("col")
    local_rows, local_cols = trailing.shape
    part = panel.shape[1]
    col_index = lax.axis_index("col")
    tile_cols = local_cols // TILE_COLS
    tiles_dev = (local_rows // TILE_ROWS) * tile_cols
    bm = 768 if local_rows % 768 == 0 else local_rows
    bn = 1024
    n_i, n_j = local_rows // bm, local_cols // bn

    row_index = lax.axis_index("row")
    place = jnp.stack([row_index, col_index]).astype(jnp.int32)
    ringed = row_devices == 8 and col_devices == 4
    if ringed:
        half = local_rows // 2
        ring = list(NEXT.items())
        parts = [(panel[:half], panel[half:])]
        for _ in range(3):
            parts.append(tuple(lax.ppermute(x, "col", ring) for x in parts[-1]))
        quarter = local_rows // 4
        spread = lax.all_to_all(
            panel.reshape(4, quarter, part),
            "row",
            split_axis=0,
            concat_axis=0,
            axis_index_groups=[[0, 2, 4, 6], [1, 3, 5, 7]],
            tiled=True,
        )
        spread, first = lax.optimization_barrier((spread, parts[1]))
        wanted = lax.all_to_all(spread, "col", split_axis=0, concat_axis=0, tiled=True)
        wanted, second, agg_vals, agg_dest, agg_tile = lax.optimization_barrier(
            (wanted, parts[2], agg_vals, agg_dest, agg_tile)
        )
        siblings = [(p, p ^ 1) for p in range(row_devices)]
        pieces, plan = [], []
        turns = ((NEXT, 1), (PREV, -1))
        for h, piece in enumerate(pair_factor(diag_inverse, wanted, quarter)):
            step, sign = turns[h]
            turn = [(2 * c + m, 2 * step[c] + m) for c in range(4) for m in range(2)]
            for n in range(4):
                if n > 0:
                    piece = lax.ppermute(piece, "row", turn)
                plan += [(h, sign * n, 0), (h, sign * n, 1)]
                pieces += [piece, lax.ppermute(piece, "row", siblings)]
        own = [panel] + [x for halves in [first, second, parts[3]] for x in halves]
        own_plan = [(0, 0, local_rows)]
        own_plan += [(s, r * half, half) for s in range(1, 4) for r in range(2)]
    else:
        whole = lax.all_gather(panel, "col", axis=0)
        column = lax.all_gather(panel, "row", axis=0, tiled=True)
        column = column.reshape(col_devices, local_cols, part)
        partner = lax.all_to_all(column, "col", split_axis=0, concat_axis=0, tiled=True)
        pieces, plan = pair_factor(diag_inverse, partner, 768), [(0, 0, 0), (1, 0, 0)]
        own = [whole[s] for s in range(col_devices)]
        own_plan = [(s, 0, local_rows) for s in range(col_devices)]

    agg, landing = exchange_tiles(agg_vals, agg_dest, agg_tile, tiles_dev)
    entries, starts = order_tiles(
        landing, row_devices * CAP, tiles_dev, tile_cols, bm, bn, n_i, n_j
    )
    rows_step = 512 if local_rows % 512 == 0 else local_rows
    halves, own_block = own_factor(
        place, diag_inverse, own, own_plan, ringed, local_rows, rows_step
    )
    updated = front(
        place, entries, starts, agg, halves, trailing, pieces, plan, ringed, bm, bn
    )
    return updated, own_block


def solution(mesh):
    in_specs = (
        P(),
        P("row", "col"),
        P("row", "col"),
        P("row", "col", None, None),
        P("row", "col", None, None),
        P("row", "col", None),
    )
    out_specs = (P("row", "col"), P("row", "col"))
    return jax.shard_map(
        per_device, mesh=mesh, in_specs=in_specs, out_specs=out_specs, check_vma=False
    )
```

```python
import functools

import jax
import jax.numpy as jnp
from jax import lax
from jax.experimental import pallas as pl
from jax.experimental.pallas import tpu as pltpu
from jax.sharding import PartitionSpec as P

TILE_ROWS = 8
TILE_COLS = 128
CAP = 2
VMEM_LIMIT = 58 << 20
NEXT = {0: 1, 1: 3, 3: 2, 2: 0}
PREV = {v: k for k, v in NEXT.items()}
NN = (((1,), (0,)), ((), ()))
NT = (((1,), (1,)), ((), ()))


def split(x):
    hi = x.astype(jnp.bfloat16)
    lo = (x - hi.astype(jnp.float32)).astype(jnp.bfloat16)
    return hi, lo


def ring_place(index, steps):
    at = (index ^ (index >> 1)) - steps & 3
    return at ^ (at >> 1)


def own_kernel(ringed, plan, rows_step, place_ref, d_ref, *refs):
    pieces = refs[: len(plan)]
    halves_ref, block_ref, stage, dtcat, full_ref, sem = refs[len(plan) :]
    width = d_ref.shape[0]
    part = stage.shape[1] // 4
    todo = []
    for n, (s, row, rows) in enumerate(plan):
        source = ring_place(place_ref[1], s) if ringed else s
        lanes = pl.ds(pl.multiple_of(source * part, part), part)
        todo.append(
            pltpu.make_async_copy(pieces[n], stage.at[pl.ds(row, rows), lanes], sem.at[n])
        )
    for c in todo:
        c.start()
    hi, lo = split(d_ref[...].T)
    dtcat[0:width, :] = hi
    dtcat[width : 2 * width, :] = hi
    dtcat[2 * width :, :] = lo
    for c in todo:
        c.wait()
    mine = pl.ds(pl.multiple_of(place_ref[1] * part, part), part)

    def body(n, carry):
        at = pl.ds(pl.multiple_of(n * rows_step, rows_step), rows_step)
        hi, lo = split(stage[at, :])
        lhs = jnp.concatenate([hi, lo, hi], axis=1)
        full = lax.dot_general(lhs, dtcat[...], NN, preferred_element_type=jnp.float32)
        full_ref[...] = full
        block_ref[at, :] = full_ref[:, mine]
        hi, lo = split(full)
        halves_ref[at, 0:width] = hi
        halves_ref[at, width:] = lo
        return carry

    lax.fori_loop(0, stage.shape[0] // rows_step, body, 0)


def own_factor(place, d, pieces, plan, ringed, rows, rows_step):
    width = d.shape[0]
    part = width // 4
    whole = pl.BlockSpec(memory_space=pltpu.VMEM)
    return pl.pallas_call(
        functools.partial(own_kernel, ringed, plan, rows_step),
        out_shape=(
            jax.ShapeDtypeStruct((rows, 2 * width), jnp.bfloat16),
            jax.ShapeDtypeStruct((rows, part), jnp.float32),
        ),
        in_specs=[pl.BlockSpec(memory_space=pltpu.SMEM), whole]
        + [pl.BlockSpec(memory_space=pl.ANY)] * len(pieces),
        out_specs=(whole, whole),
        scratch_shapes=[
            pltpu.VMEM((rows, width), jnp.float32),
            pltpu.VMEM((3 * width, width), jnp.bfloat16),
            pltpu.VMEM((rows_step, width), jnp.float32),
            pltpu.SemaphoreType.DMA((len(pieces),)),
        ],
        compiler_params=pltpu.CompilerParams(vmem_limit_bytes=VMEM_LIMIT),
        cost_estimate=pl.CostEstimate(
            flops=6 * rows * width * width, bytes_accessed=10 * rows * width, transcendentals=0
        ),
        name="own_factor",
    )(place, d, *pieces)


def pair_kernel(d_ref, panel_ref, top_ref, low_ref):
    width = d_ref.shape[0]
    half = width // 2
    d_hi, d_lo = split(d_ref[...])
    hi, lo = split(jnp.concatenate([panel_ref[s] for s in range(4)], axis=1))
    for ref, rows, upto in ((top_ref, slice(0, half), half), (low_ref, slice(half, width), width)):
        d_rows = d_hi[rows, :upto]
        lhs = jnp.concatenate([d_rows, d_rows, d_lo[rows, :upto]], axis=1)
        rhs = jnp.concatenate([hi[:, :upto], lo[:, :upto], hi[:, :upto]], axis=1)
        ref[...] = lax.dot_general(lhs, rhs, NT, preferred_element_type=jnp.float32)


def pair_factor(d, panel, rows_step):
    width = d.shape[0]
    parts, rows, part = panel.shape
    out = jax.ShapeDtypeStruct((width // 2, rows), jnp.float32)
    out_block = pl.BlockSpec((width // 2, rows_step), lambda n: (0, n))
    return pl.pallas_call(
        pair_kernel,
        grid=(rows // rows_step,),
        out_shape=(out, out),
        in_specs=[
            pl.BlockSpec((width, width), lambda n: (0, 0)),
            pl.BlockSpec((parts, rows_step, part), lambda n: (0, n, 0)),
        ],
        out_specs=(out_block, out_block),
        compiler_params=pltpu.CompilerParams(vmem_limit_bytes=VMEM_LIMIT),
        cost_estimate=pl.CostEstimate(
            flops=6 * rows * width * width, bytes_accessed=8 * rows * width, transcendentals=0
        ),
        name="pair_factor",
    )(d, panel)


def front_kernel(
    ringed, plan, place_ref, entry_ref, start_ref, agg_ref, own_ref, trail_ref, *refs
):
    pieces = refs[: len(plan)]
    out_ref, stage, pair_cat, sem = refs[len(plan) :]
    j, i = pl.program_id(0), pl.program_id(1)
    n_i = pl.num_programs(1)
    bm, bn = out_ref.shape
    width = stage.shape[0]

    @pl.when((i == 0) & (j == 0))
    def _():
        todo = []
        for n, (half, steps, swap) in enumerate(plan):
            depth, cols = pieces[n].shape
            block = 0
            if ringed:
                chip = ring_place(place_ref[0] // 2, steps)
                block = (place_ref[0] % 2 ^ swap) * 4 + chip
            at = pl.ds(pl.multiple_of(block * cols, TILE_COLS), cols)
            rows = pl.ds(half * depth, depth)
            todo.append(pltpu.make_async_copy(pieces[n], stage.at[rows, at], sem.at[n]))
        for c in todo:
            c.start()
        for c in todo:
            c.wait()

    @pl.when(i == 0)
    def _():
        cols = pl.ds(pl.multiple_of(j * bn, bn), bn)
        hi, lo = split(stage[:, cols])
        pair_cat[0:width, :] = hi
        pair_cat[width : 2 * width, :] = lo
        pair_cat[2 * width :, :] = hi

    rows = pl.ds(pl.multiple_of(i * bm, bm), bm)
    hi, lo = own_ref[rows, 0:width], own_ref[rows, width:]
    lhs = jnp.concatenate([hi, hi, lo], axis=1)
    for n in range(0, bn, 256):
        at = slice(n, n + 256)
        product = lax.dot_general(lhs, pair_cat[:, at], NN, preferred_element_type=jnp.float32)
        out_ref[:, at] = trail_ref[:, at] - product
    step = j * n_i + i

    def add(e, carry):
        r = pl.multiple_of(entry_ref[1, e], TILE_ROWS)
        c = pl.multiple_of(entry_ref[2, e], TILE_COLS)
        here = (pl.ds(r, TILE_ROWS), pl.ds(c, TILE_COLS))
        out_ref[here] = out_ref[here] + agg_ref[entry_ref[0, e]]
        return carry

    lax.fori_loop(start_ref[step], start_ref[step + 1], add, 0)


def front(place, entries, starts, agg, own, trailing, pieces, plan, ringed, bm, bn):
    rows, cols = trailing.shape
    width = own.shape[1] // 2
    whole = pl.BlockSpec(memory_space=pltpu.VMEM)
    smem = pl.BlockSpec(memory_space=pltpu.SMEM)
    block = pl.BlockSpec((bm, bn), lambda j, i: (i, j))
    return pl.pallas_call(
        functools.partial(front_kernel, ringed, plan),
        grid=(cols // bn, rows // bm),
        out_shape=jax.ShapeDtypeStruct((rows, cols), jnp.float32),
        in_specs=[smem, smem, smem, whole, whole, block]
        + [pl.BlockSpec(memory_space=pl.ANY)] * len(pieces),
        out_specs=block,
        scratch_shapes=[
            pltpu.VMEM((width, cols), jnp.float32),
            pltpu.VMEM((3 * width, bn), jnp.bfloat16),
            pltpu.SemaphoreType.DMA((len(pieces),)),
        ],
        compiler_params=pltpu.CompilerParams(vmem_limit_bytes=VMEM_LIMIT),
        cost_estimate=pl.CostEstimate(
            flops=6 * rows * width * cols,
            bytes_accessed=8 * rows * cols + 4 * width * cols,
            transcendentals=0,
        ),
        name="front",
    )(place, entries, starts, agg, own, trailing, *pieces)


def pack_tiles(agg_vals, agg_dest, agg_tile, tiles_dev):
    row_devices = lax.axis_size("row")
    agg = agg_vals.shape[2]
    targets = agg_dest.reshape(-1)
    tile_ids = agg_tile.reshape(-1)
    slots = row_devices * CAP
    order = jnp.arange(agg, dtype=jnp.int32)
    earlier = (targets[None, :] == targets[:, None]) & (order[None, :] < order[:, None])
    position = targets * CAP + jnp.sum(earlier.astype(jnp.int32), axis=1)
    hit = position[None, :] == jnp.arange(slots, dtype=jnp.int32)[:, None]
    send_ids = tiles_dev + jnp.sum(jnp.where(hit, tile_ids[None, :] - tiles_dev, 0), axis=1)
    values = agg_vals.reshape(agg, TILE_ROWS, TILE_COLS)
    send = jnp.zeros((slots, TILE_ROWS, TILE_COLS), jnp.float32).at[position].set(values)
    send = send.reshape(row_devices, CAP, TILE_ROWS, TILE_COLS)
    numbers = send_ids.astype(jnp.float32).reshape(row_devices, 1, 1, CAP)
    numbers = jnp.pad(numbers, ((0, 0), (0, 0), (0, TILE_ROWS - 1), (0, TILE_COLS - CAP)))
    return jnp.concatenate([send, numbers], axis=1)


def exchange_tiles(send, tiles_dev):
    got = lax.all_to_all(send, "row", split_axis=0, concat_axis=0, tiled=True)
    landing = got[:, CAP, 0, :CAP].astype(jnp.int32)
    landing = jnp.pad(landing, ((0, 0), (0, 1)), constant_values=tiles_dev)
    return got.reshape(-1, TILE_ROWS, TILE_COLS), landing.reshape(-1)


def order_tiles(landing, slots, tiles_dev, tile_cols, bm, bn, n_i, n_j):
    row = (landing // tile_cols) * TILE_ROWS
    col = (landing % tile_cols) * TILE_COLS
    count = landing.shape[0]
    number = jnp.arange(count, dtype=jnp.int32)
    step = jnp.where(landing < tiles_dev, (col // bn) * n_i + row // bm, n_i * n_j)
    key = step * count + number
    rank = jnp.sum((key[None, :] < key[:, None]).astype(jnp.int32), axis=1)
    hit = (rank[None, :] == jnp.arange(slots, dtype=jnp.int32)[:, None]).astype(jnp.int32)
    fields = jnp.stack([number, row % bm, col % bn])
    entries = jnp.sum(hit[None] * fields[:, None, :], axis=2)
    edges = jnp.arange(n_i * n_j + 1, dtype=jnp.int32)
    starts = jnp.sum((step[None, :] < edges[:, None]).astype(jnp.int32), axis=1)
    return entries, starts


def per_device(diag_inverse, panel, trailing, agg_vals, agg_dest, agg_tile):
    row_devices = lax.axis_size("row")
    col_devices = lax.axis_size("col")
    local_rows, local_cols = trailing.shape
    part = panel.shape[1]
    col_index = lax.axis_index("col")
    tile_cols = local_cols // TILE_COLS
    tiles_dev = (local_rows // TILE_ROWS) * tile_cols
    bm = 768 if local_rows % 768 == 0 else local_rows
    bn = 1024
    n_i, n_j = local_rows // bm, local_cols // bn

    row_index = lax.axis_index("row")
    place = jnp.stack([row_index, col_index]).astype(jnp.int32)
    tiles = pack_tiles(agg_vals, agg_dest, agg_tile, tiles_dev)
    ringed = row_devices == 8 and col_devices == 4
    if ringed:
        half = local_rows // 2
        ring = list(NEXT.items())
        parts = [(panel[:half], panel[half:])]
        for _ in range(3):
            parts.append(tuple(lax.ppermute(x, "col", ring) for x in parts[-1]))
        quarter = local_rows // 4
        spread = lax.all_to_all(
            panel.reshape(4, quarter, part),
            "row",
            split_axis=0,
            concat_axis=0,
            axis_index_groups=[[0, 2, 4, 6], [1, 3, 5, 7]],
            tiled=True,
        )
        spread, first, tiles = lax.optimization_barrier((spread, parts[1][0], tiles))
        wanted = lax.all_to_all(spread, "col", split_axis=0, concat_axis=0, tiled=True)
        wanted, second = lax.optimization_barrier((wanted, parts[2][0]))
        siblings = [(p, p ^ 1) for p in range(row_devices)]
        pieces, plan, across = [], [], []
        turns = ((NEXT, 1), (PREV, -1))
        for h, piece in enumerate(pair_factor(diag_inverse, wanted, quarter)):
            step, sign = turns[h]
            turn = [(2 * c + m, 2 * step[c] + m) for c in range(4) for m in range(2)]
            for n in range(4):
                if n > 0:
                    piece = lax.ppermute(piece, "row", turn)
                if n == 2:
                    across.append(piece)
                plan += [(h, sign * n, 0), (h, sign * n, 1)]
                pieces += [piece, lax.ppermute(piece, "row", siblings)]
        last, across = lax.optimization_barrier((parts[3], tuple(across)))
        pieces[4], pieces[12] = across
        own = [panel, first, parts[1][1], second, parts[2][1], *last]
        own_plan = [(0, 0, local_rows)]
        own_plan += [(s, r * half, half) for s in range(1, 4) for r in range(2)]
    else:
        whole = lax.all_gather(panel, "col", axis=0)
        column = lax.all_gather(panel, "row", axis=0, tiled=True)
        column = column.reshape(col_devices, local_cols, part)
        partner = lax.all_to_all(column, "col", split_axis=0, concat_axis=0, tiled=True)
        pieces, plan = pair_factor(diag_inverse, partner, 768), [(0, 0, 0), (1, 0, 0)]
        own = [whole[s] for s in range(col_devices)]
        own_plan = [(s, 0, local_rows) for s in range(col_devices)]

    agg, landing = exchange_tiles(tiles, tiles_dev)
    entries, starts = order_tiles(
        landing, row_devices * CAP, tiles_dev, tile_cols, bm, bn, n_i, n_j
    )
    rows_step = 512 if local_rows % 512 == 0 else local_rows
    halves, own_block = own_factor(
        place, diag_inverse, own, own_plan, ringed, local_rows, rows_step
    )
    updated = front(
        place, entries, starts, agg, halves, trailing, pieces, plan, ringed, bm, bn
    )
    return updated, own_block


def solution(mesh):
    in_specs = (
        P(),
        P("row", "col"),
        P("row", "col"),
        P("row", "col", None, None),
        P("row", "col", None, None),
        P("row", "col", None),
    )
    out_specs = (P("row", "col"), P("row", "col"))
    return jax.shard_map(
        per_device, mesh=mesh, in_specs=in_specs, out_specs=out_specs, check_vma=False
    )
```

```python
import functools

import jax
import jax.numpy as jnp
from jax import lax
from jax.experimental import pallas as pl
from jax.experimental.pallas import tpu as pltpu
from jax.sharding import PartitionSpec as P

TILE_ROWS = 8
TILE_COLS = 128
CAP = 2
VMEM_LIMIT = 58 << 20
NEXT = {0: 1, 1: 3, 3: 2, 2: 0}
PREV = {v: k for k, v in NEXT.items()}
NN = (((1,), (0,)), ((), ()))
NT = (((1,), (1,)), ((), ()))


def split(x):
    hi = x.astype(jnp.bfloat16)
    lo = (x - hi.astype(jnp.float32)).astype(jnp.bfloat16)
    return hi, lo


def ring_place(index, steps):
    at = (index ^ (index >> 1)) - steps & 3
    return at ^ (at >> 1)


def pair_kernel(d_ref, panel_ref, top_ref, low_ref):
    width = d_ref.shape[0]
    half = width // 2
    d_hi, d_lo = split(d_ref[...])
    hi, lo = split(jnp.concatenate([panel_ref[s] for s in range(4)], axis=1))
    for ref, rows, upto in ((top_ref, slice(0, half), half), (low_ref, slice(half, width), width)):
        d_rows = d_hi[rows, :upto]
        lhs = jnp.concatenate([d_rows, d_rows, d_lo[rows, :upto]], axis=1)
        rhs = jnp.concatenate([hi[:, :upto], lo[:, :upto], hi[:, :upto]], axis=1)
        ref[...] = lax.dot_general(lhs, rhs, NT, preferred_element_type=jnp.float32)


def pair_factor(d, panel, rows_step):
    width = d.shape[0]
    parts, rows, part = panel.shape
    out = jax.ShapeDtypeStruct((width // 2, rows), jnp.float32)
    out_block = pl.BlockSpec((width // 2, rows_step), lambda n: (0, n))
    return pl.pallas_call(
        pair_kernel,
        grid=(rows // rows_step,),
        out_shape=(out, out),
        in_specs=[
            pl.BlockSpec((width, width), lambda n: (0, 0)),
            pl.BlockSpec((parts, rows_step, part), lambda n: (0, n, 0)),
        ],
        out_specs=(out_block, out_block),
        compiler_params=pltpu.CompilerParams(vmem_limit_bytes=VMEM_LIMIT),
        cost_estimate=pl.CostEstimate(
            flops=6 * rows * width * width, bytes_accessed=8 * rows * width, transcendentals=0
        ),
        name="pair_factor",
    )(d, panel)


def front_kernel(
    ringed, own_plan, plan, place_ref, entry_ref, start_ref, d_ref, agg_ref, trail_ref, *refs
):
    n_own, n_pair = len(own_plan), len(plan)
    own_pieces, pieces = refs[:n_own], refs[n_own : n_own + n_pair]
    out_ref, block_ref = refs[n_own + n_pair : n_own + n_pair + 2]
    own_stage, stage, dt_left, dt_right, own_cat, pair_cat, full, sem = refs[n_own + n_pair + 2 :]
    j, i = pl.program_id(0), pl.program_id(1)
    n_i = pl.num_programs(1)
    bm, bn = out_ref.shape
    width = d_ref.shape[0]
    half = width // 2
    part = width // 4

    @pl.when((i == 0) & (j == 0))
    def _():
        todo = []
        for n, s in enumerate(own_plan):
            source = ring_place(place_ref[1], s) if ringed else s
            lanes = pl.ds(pl.multiple_of(source * part, part), part)
            todo.append(pltpu.make_async_copy(own_pieces[n], own_stage.at[:, lanes], sem.at[n]))
        for n, (upper, steps, swap) in enumerate(plan):
            depth, cols = pieces[n].shape
            block = 0
            if ringed:
                chip = ring_place(place_ref[0] // 2, steps)
                block = (place_ref[0] % 2 ^ swap) * 4 + chip
            at = pl.ds(pl.multiple_of(block * cols, TILE_COLS), cols)
            rows = pl.ds(upper * depth, depth)
            todo.append(
                pltpu.make_async_copy(pieces[n], stage.at[rows, at], sem.at[n_own + n])
            )
        for c in todo:
            c.start()
        hi, lo = split(d_ref[...].T)
        dt_left[...] = jnp.concatenate(
            [hi[:half, :half], hi[:half, :half], lo[:half, :half]], axis=0
        )
        dt_right[...] = jnp.concatenate([hi[:, half:], hi[:, half:], lo[:, half:]], axis=0)
        for c in todo:
            c.wait()

    rows = pl.ds(pl.multiple_of(i * bm, bm), bm)

    @pl.when(j == 0)
    def _():
        hi, lo = split(own_stage[rows, :])
        lhs = jnp.concatenate([hi[:, :half], lo[:, :half], hi[:, :half]], axis=1)
        full[:, :half] = lax.dot_general(
            lhs, dt_left[...], NN, preferred_element_type=jnp.float32
        )
        lhs = jnp.concatenate([hi, lo, hi], axis=1)
        full[:, half:] = lax.dot_general(
            lhs, dt_right[...], NN, preferred_element_type=jnp.float32
        )
        block_ref[...] = full[:, pl.ds(pl.multiple_of(place_ref[1] * part, part), part)]
        hi, lo = split(full[...])
        own_cat[rows, :] = jnp.concatenate([hi, hi, lo], axis=1)

    @pl.when(i == 0)
    def _():
        cols = pl.ds(pl.multiple_of(j * bn, bn), bn)
        hi, lo = split(stage[:, cols])
        pair_cat[0:width, :] = hi
        pair_cat[width : 2 * width, :] = lo
        pair_cat[2 * width :, :] = hi

    for n in range(0, bn, 256):
        at = slice(n, n + 256)
        product = lax.dot_general(
            own_cat[rows, :], pair_cat[:, at], NN, preferred_element_type=jnp.float32
        )
        out_ref[:, at] = trail_ref[:, at] - product
    step = j * n_i + i

    def add(e, carry):
        r = pl.multiple_of(entry_ref[1, e], TILE_ROWS)
        c = pl.multiple_of(entry_ref[2, e], TILE_COLS)
        here = (pl.ds(r, TILE_ROWS), pl.ds(c, TILE_COLS))
        out_ref[here] = out_ref[here] + agg_ref[entry_ref[0, e]]
        return carry

    lax.fori_loop(start_ref[step], start_ref[step + 1], add, 0)


def front(place, entries, starts, d, agg, trailing, own, own_plan, pieces, plan, ringed, bm, bn):
    rows, cols = trailing.shape
    width = d.shape[0]
    half, part = width // 2, width // 4
    n_i = rows // bm
    whole = pl.BlockSpec(memory_space=pltpu.VMEM)
    smem = pl.BlockSpec(memory_space=pltpu.SMEM)
    block = pl.BlockSpec((bm, bn), lambda j, i: (i, j))
    operands = len(own) + len(pieces)
    return pl.pallas_call(
        functools.partial(front_kernel, ringed, own_plan, plan),
        grid=(cols // bn, n_i),
        out_shape=(
            jax.ShapeDtypeStruct((rows, cols), jnp.float32),
            jax.ShapeDtypeStruct((rows, part), jnp.float32),
        ),
        in_specs=[smem, smem, smem, whole, whole, block]
        + [pl.BlockSpec(memory_space=pl.ANY)] * operands,
        out_specs=(
            block,
            pl.BlockSpec((bm, part), lambda j, i: (jnp.where(j == 0, i, n_i - 1), 0)),
        ),
        scratch_shapes=[
            pltpu.VMEM((rows, width), jnp.float32),
            pltpu.VMEM((width, cols), jnp.float32),
            pltpu.VMEM((3 * half, half), jnp.bfloat16),
            pltpu.VMEM((3 * width, half), jnp.bfloat16),
            pltpu.VMEM((rows, 3 * width), jnp.bfloat16),
            pltpu.VMEM((3 * width, bn), jnp.bfloat16),
            pltpu.VMEM((bm, width), jnp.float32),
            pltpu.SemaphoreType.DMA((operands,)),
        ],
        compiler_params=pltpu.CompilerParams(vmem_limit_bytes=VMEM_LIMIT),
        cost_estimate=pl.CostEstimate(
            flops=6 * rows * width * (cols + width),
            bytes_accessed=8 * rows * cols + 4 * width * cols,
            transcendentals=0,
        ),
        name="front",
    )(place, entries, starts, d, agg, trailing, *own, *pieces)


def pack_tiles(agg_vals, agg_dest, agg_tile, tiles_dev):
    row_devices = lax.axis_size("row")
    agg = agg_vals.shape[2]
    targets = agg_dest.reshape(-1)
    tile_ids = agg_tile.reshape(-1)
    slots = row_devices * CAP
    order = jnp.arange(agg, dtype=jnp.int32)
    earlier = (targets[None, :] == targets[:, None]) & (order[None, :] < order[:, None])
    position = targets * CAP + jnp.sum(earlier.astype(jnp.int32), axis=1)
    hit = position[None, :] == jnp.arange(slots, dtype=jnp.int32)[:, None]
    send_ids = tiles_dev + jnp.sum(jnp.where(hit, tile_ids[None, :] - tiles_dev, 0), axis=1)
    values = agg_vals.reshape(agg, TILE_ROWS, TILE_COLS)
    send = jnp.zeros((slots, TILE_ROWS, TILE_COLS), jnp.float32).at[position].set(values)
    send = send.reshape(row_devices, CAP, TILE_ROWS, TILE_COLS)
    numbers = send_ids.astype(jnp.float32).reshape(row_devices, 1, 1, CAP)
    numbers = jnp.pad(numbers, ((0, 0), (0, 0), (0, TILE_ROWS - 1), (0, TILE_COLS - CAP)))
    return jnp.concatenate([send, numbers], axis=1)


def exchange_tiles(send, tiles_dev):
    got = lax.all_to_all(send, "row", split_axis=0, concat_axis=0, tiled=True)
    landing = got[:, CAP, 0, :CAP].astype(jnp.int32)
    landing = jnp.pad(landing, ((0, 0), (0, 1)), constant_values=tiles_dev)
    return got.reshape(-1, TILE_ROWS, TILE_COLS), landing.reshape(-1)


def order_tiles(landing, slots, tiles_dev, tile_cols, bm, bn, n_i, n_j):
    row = (landing // tile_cols) * TILE_ROWS
    col = (landing % tile_cols) * TILE_COLS
    count = landing.shape[0]
    number = jnp.arange(count, dtype=jnp.int32)
    step = jnp.where(landing < tiles_dev, (col // bn) * n_i + row // bm, n_i * n_j)
    key = step * count + number
    rank = jnp.sum((key[None, :] < key[:, None]).astype(jnp.int32), axis=1)
    hit = (rank[None, :] == jnp.arange(slots, dtype=jnp.int32)[:, None]).astype(jnp.int32)
    fields = jnp.stack([number, row % bm, col % bn])
    entries = jnp.sum(hit[None] * fields[:, None, :], axis=2)
    edges = jnp.arange(n_i * n_j + 1, dtype=jnp.int32)
    starts = jnp.sum((step[None, :] < edges[:, None]).astype(jnp.int32), axis=1)
    return entries, starts


def per_device(diag_inverse, panel, trailing, agg_vals, agg_dest, agg_tile):
    row_devices = lax.axis_size("row")
    col_devices = lax.axis_size("col")
    local_rows, local_cols = trailing.shape
    part = panel.shape[1]
    col_index = lax.axis_index("col")
    tile_cols = local_cols // TILE_COLS
    tiles_dev = (local_rows // TILE_ROWS) * tile_cols
    bm = 768 if local_rows % 768 == 0 else local_rows
    bn = 1024
    n_i, n_j = local_rows // bm, local_cols // bn

    row_index = lax.axis_index("row")
    place = jnp.stack([row_index, col_index]).astype(jnp.int32)
    tiles = pack_tiles(agg_vals, agg_dest, agg_tile, tiles_dev)
    ringed = row_devices == 8 and col_devices == 4
    if ringed:
        quarter = local_rows // 4
        ring = functools.partial(lax.ppermute, axis_name="col", perm=list(NEXT.items()))
        spread = lax.all_to_all(
            panel.reshape(4, quarter, part),
            "row",
            split_axis=0,
            concat_axis=0,
            axis_index_groups=[[0, 2, 4, 6], [1, 3, 5, 7]],
            tiled=True,
        )
        spread, first, tiles = lax.optimization_barrier((spread, ring(panel), tiles))
        wanted = lax.all_to_all(spread, "col", split_axis=0, concat_axis=0, tiled=True)
        wanted, first, tiles = lax.optimization_barrier((wanted, first, tiles))
        second = ring(first)
        siblings = [(p, p ^ 1) for p in range(row_devices)]
        pieces, plan = [], []
        turns = ((NEXT, 1), (PREV, -1))
        for h, piece in enumerate(pair_factor(diag_inverse, wanted, quarter)):
            step, sign = turns[h]
            turn = [(2 * c + m, 2 * step[c] + m) for c in range(4) for m in range(2)]
            for n in range(4):
                if n > 0:
                    piece = lax.ppermute(piece, "row", turn)
                plan += [(h, sign * n, 0), (h, sign * n, 1)]
                pieces += [piece, lax.ppermute(piece, "row", siblings)]
        own = [panel, first, second, ring(second)]
    else:
        whole = lax.all_gather(panel, "col", axis=0)
        column = lax.all_gather(panel, "row", axis=0, tiled=True)
        column = column.reshape(col_devices, local_cols, part)
        partner = lax.all_to_all(column, "col", split_axis=0, concat_axis=0, tiled=True)
        pieces, plan = pair_factor(diag_inverse, partner, 768), [(0, 0, 0), (1, 0, 0)]
        own = [whole[s] for s in range(col_devices)]

    agg, landing = exchange_tiles(tiles, tiles_dev)
    entries, starts = order_tiles(
        landing, row_devices * CAP, tiles_dev, tile_cols, bm, bn, n_i, n_j
    )
    return front(
        place,
        entries,
        starts,
        diag_inverse,
        agg,
        trailing,
        own,
        list(range(4)),
        pieces,
        plan,
        ringed,
        bm,
        bn,
    )


def solution(mesh):
    in_specs = (
        P(),
        P("row", "col"),
        P("row", "col"),
        P("row", "col", None, None),
        P("row", "col", None, None),
        P("row", "col", None),
    )
    out_specs = (P("row", "col"), P("row", "col"))
    return jax.shard_map(
        per_device, mesh=mesh, in_specs=in_specs, out_specs=out_specs, check_vma=False
    )
```

```python
import functools

import jax
import jax.numpy as jnp
from jax import lax
from jax.experimental import pallas as pl
from jax.experimental.pallas import tpu as pltpu
from jax.sharding import PartitionSpec as P

TILE_ROWS = 8
TILE_COLS = 128
CAP = 2
VMEM_LIMIT = 58 << 20
NEXT = {0: 1, 1: 3, 3: 2, 2: 0}
PREV = {v: k for k, v in NEXT.items()}
NN = (((1,), (0,)), ((), ()))
NT = (((1,), (1,)), ((), ()))


def split(x):
    hi = x.astype(jnp.bfloat16)
    lo = (x - hi.astype(jnp.float32)).astype(jnp.bfloat16)
    return hi, lo


def ring_place(index, steps):
    at = (index ^ (index >> 1)) - steps & 3
    return at ^ (at >> 1)


def pair_kernel(d_ref, panel_ref, top_ref, low_ref):
    width = d_ref.shape[0]
    half = width // 2
    d_hi, d_lo = split(d_ref[...])
    hi, lo = split(jnp.concatenate([panel_ref[s] for s in range(4)], axis=1))
    for ref, rows, upto in ((top_ref, slice(0, half), half), (low_ref, slice(half, width), width)):
        d_rows = d_hi[rows, :upto]
        lhs = jnp.concatenate([d_rows, d_rows, d_lo[rows, :upto]], axis=1)
        rhs = jnp.concatenate([hi[:, :upto], lo[:, :upto], hi[:, :upto]], axis=1)
        ref[...] = lax.dot_general(lhs, rhs, NT, preferred_element_type=jnp.float32)


def pair_factor(d, panel, rows_step):
    width = d.shape[0]
    parts, rows, part = panel.shape
    out = jax.ShapeDtypeStruct((width // 2, rows), jnp.float32)
    out_block = pl.BlockSpec((width // 2, rows_step), lambda n: (0, n))
    return pl.pallas_call(
        pair_kernel,
        grid=(rows // rows_step,),
        out_shape=(out, out),
        in_specs=[
            pl.BlockSpec((width, width), lambda n: (0, 0)),
            pl.BlockSpec((parts, rows_step, part), lambda n: (0, n, 0)),
        ],
        out_specs=(out_block, out_block),
        compiler_params=pltpu.CompilerParams(vmem_limit_bytes=VMEM_LIMIT),
        cost_estimate=pl.CostEstimate(
            flops=6 * rows * width * width, bytes_accessed=8 * rows * width, transcendentals=0
        ),
        name="pair_factor",
    )(d, panel)


def front_kernel(
    ringed, own_plan, plan, place_ref, entry_ref, start_ref, d_ref, agg_ref, trail_ref, *refs
):
    n_own, n_pair = len(own_plan), len(plan)
    own_pieces, pieces = refs[:n_own], refs[n_own : n_own + n_pair]
    out_ref, block_ref = refs[n_own + n_pair : n_own + n_pair + 2]
    own_stage, stage, dt_left, dt_right, own_cat, pair_cat, full, sem = refs[n_own + n_pair + 2 :]
    j, i = pl.program_id(0), pl.program_id(1)
    n_i = pl.num_programs(1)
    bm, bn = out_ref.shape
    width = d_ref.shape[0]
    half = width // 2
    part = width // 4

    @pl.when((i == 0) & (j == 0))
    def _():
        todo = []
        for n, s in enumerate(own_plan):
            source = ring_place(place_ref[1], s) if ringed else s
            lanes = pl.ds(pl.multiple_of(source * part, part), part)
            todo.append(pltpu.make_async_copy(own_pieces[n], own_stage.at[:, lanes], sem.at[n]))
        for n, (upper, steps, swap) in enumerate(plan):
            depth, cols = pieces[n].shape
            block = 0
            if ringed:
                chip = ring_place(place_ref[0] // 2, steps)
                block = (place_ref[0] % 2 ^ swap) * 4 + chip
            at = pl.ds(pl.multiple_of(block * cols, TILE_COLS), cols)
            rows = pl.ds(upper * depth, depth)
            todo.append(
                pltpu.make_async_copy(pieces[n], stage.at[rows, at], sem.at[n_own + n])
            )
        for c in todo:
            c.start()
        hi, lo = split(d_ref[...].T)
        dt_left[...] = jnp.concatenate(
            [hi[:half, :half], hi[:half, :half], lo[:half, :half]], axis=0
        )
        dt_right[...] = jnp.concatenate([hi[:, half:], hi[:, half:], lo[:, half:]], axis=0)
        for c in todo:
            c.wait()

    rows = pl.ds(pl.multiple_of(i * bm, bm), bm)

    @pl.when(j == 0)
    def _():
        hi, lo = split(own_stage[rows, :])
        lhs = jnp.concatenate([hi[:, :half], lo[:, :half], hi[:, :half]], axis=1)
        full[:, :half] = lax.dot_general(
            lhs, dt_left[...], NN, preferred_element_type=jnp.float32
        )
        lhs = jnp.concatenate([hi, lo, hi], axis=1)
        full[:, half:] = lax.dot_general(
            lhs, dt_right[...], NN, preferred_element_type=jnp.float32
        )
        block_ref[...] = full[:, pl.ds(pl.multiple_of(place_ref[1] * part, part), part)]
        hi, lo = split(full[...])
        own_cat[rows, :] = jnp.concatenate([hi, hi, lo], axis=1)

    @pl.when(i == 0)
    def _():
        cols = pl.ds(pl.multiple_of(j * bn, bn), bn)
        hi, lo = split(stage[:, cols])
        pair_cat[0:width, :] = hi
        pair_cat[width : 2 * width, :] = lo
        pair_cat[2 * width :, :] = hi

    for n in range(0, bn, 256):
        at = slice(n, n + 256)
        product = lax.dot_general(
            own_cat[rows, :], pair_cat[:, at], NN, preferred_element_type=jnp.float32
        )
        out_ref[:, at] = trail_ref[:, at] - product
    step = j * n_i + i

    def add(e, carry):
        r = pl.multiple_of(entry_ref[1, e], TILE_ROWS)
        c = pl.multiple_of(entry_ref[2, e], TILE_COLS)
        here = (pl.ds(r, TILE_ROWS), pl.ds(c, TILE_COLS))
        out_ref[here] = out_ref[here] + agg_ref[entry_ref[0, e]]
        return carry

    lax.fori_loop(start_ref[step], start_ref[step + 1], add, 0)


def front(place, entries, starts, d, agg, trailing, own, own_plan, pieces, plan, ringed, bm, bn):
    rows, cols = trailing.shape
    width = d.shape[0]
    half, part = width // 2, width // 4
    n_i = rows // bm
    whole = pl.BlockSpec(memory_space=pltpu.VMEM)
    smem = pl.BlockSpec(memory_space=pltpu.SMEM)
    block = pl.BlockSpec((bm, bn), lambda j, i: (i, j))
    operands = len(own) + len(pieces)
    return pl.pallas_call(
        functools.partial(front_kernel, ringed, own_plan, plan),
        grid=(cols // bn, n_i),
        out_shape=(
            jax.ShapeDtypeStruct((rows, cols), jnp.float32),
            jax.ShapeDtypeStruct((rows, part), jnp.float32),
        ),
        in_specs=[smem, smem, smem, whole, whole, block]
        + [pl.BlockSpec(memory_space=pl.ANY)] * operands,
        out_specs=(
            block,
            pl.BlockSpec((bm, part), lambda j, i: (jnp.where(j == 0, i, n_i - 1), 0)),
        ),
        scratch_shapes=[
            pltpu.VMEM((rows, width), jnp.float32),
            pltpu.VMEM((width, cols), jnp.float32),
            pltpu.VMEM((3 * half, half), jnp.bfloat16),
            pltpu.VMEM((3 * width, half), jnp.bfloat16),
            pltpu.VMEM((rows, 3 * width), jnp.bfloat16),
            pltpu.VMEM((3 * width, bn), jnp.bfloat16),
            pltpu.VMEM((bm, width), jnp.float32),
            pltpu.SemaphoreType.DMA((operands,)),
        ],
        compiler_params=pltpu.CompilerParams(vmem_limit_bytes=VMEM_LIMIT),
        cost_estimate=pl.CostEstimate(
            flops=6 * rows * width * (cols + width),
            bytes_accessed=8 * rows * cols + 4 * width * cols,
            transcendentals=0,
        ),
        name="front",
    )(place, entries, starts, d, agg, trailing, *own, *pieces)


def pack_tiles(agg_vals, agg_dest, agg_tile, tiles_dev):
    row_devices = lax.axis_size("row")
    agg = agg_vals.shape[2]
    targets = agg_dest.reshape(-1)
    tile_ids = agg_tile.reshape(-1)
    slots = row_devices * CAP
    order = jnp.arange(agg, dtype=jnp.int32)
    earlier = (targets[None, :] == targets[:, None]) & (order[None, :] < order[:, None])
    position = targets * CAP + jnp.sum(earlier.astype(jnp.int32), axis=1)
    hit = position[None, :] == jnp.arange(slots, dtype=jnp.int32)[:, None]
    send_ids = tiles_dev + jnp.sum(jnp.where(hit, tile_ids[None, :] - tiles_dev, 0), axis=1)
    values = agg_vals.reshape(agg, TILE_ROWS, TILE_COLS)
    send = jnp.zeros((slots, TILE_ROWS, TILE_COLS), jnp.float32).at[position].set(values)
    send = send.reshape(row_devices, CAP, TILE_ROWS, TILE_COLS)
    numbers = send_ids.astype(jnp.float32).reshape(row_devices, 1, 1, CAP)
    numbers = jnp.pad(numbers, ((0, 0), (0, 0), (0, TILE_ROWS - 1), (0, TILE_COLS - CAP)))
    return jnp.concatenate([send, numbers], axis=1)


def exchange_tiles(send, tiles_dev):
    got = lax.all_to_all(send, "row", split_axis=0, concat_axis=0, tiled=True)
    landing = got[:, CAP, 0, :CAP].astype(jnp.int32)
    landing = jnp.pad(landing, ((0, 0), (0, 1)), constant_values=tiles_dev)
    return got.reshape(-1, TILE_ROWS, TILE_COLS), landing.reshape(-1)


def order_tiles(landing, slots, tiles_dev, tile_cols, bm, bn, n_i, n_j):
    row = (landing // tile_cols) * TILE_ROWS
    col = (landing % tile_cols) * TILE_COLS
    count = landing.shape[0]
    number = jnp.arange(count, dtype=jnp.int32)
    step = jnp.where(landing < tiles_dev, (col // bn) * n_i + row // bm, n_i * n_j)
    key = step * count + number
    rank = jnp.sum((key[None, :] < key[:, None]).astype(jnp.int32), axis=1)
    hit = (rank[None, :] == jnp.arange(slots, dtype=jnp.int32)[:, None]).astype(jnp.int32)
    fields = jnp.stack([number, row % bm, col % bn])
    entries = jnp.sum(hit[None] * fields[:, None, :], axis=2)
    edges = jnp.arange(n_i * n_j + 1, dtype=jnp.int32)
    starts = jnp.sum((step[None, :] < edges[:, None]).astype(jnp.int32), axis=1)
    return entries, starts


def per_device(diag_inverse, panel, trailing, agg_vals, agg_dest, agg_tile):
    row_devices = lax.axis_size("row")
    col_devices = lax.axis_size("col")
    local_rows, local_cols = trailing.shape
    part = panel.shape[1]
    col_index = lax.axis_index("col")
    tile_cols = local_cols // TILE_COLS
    tiles_dev = (local_rows // TILE_ROWS) * tile_cols
    bm = 768 if local_rows % 768 == 0 else local_rows
    bn = 1024
    n_i, n_j = local_rows // bm, local_cols // bn

    row_index = lax.axis_index("row")
    place = jnp.stack([row_index, col_index]).astype(jnp.int32)
    tiles = pack_tiles(agg_vals, agg_dest, agg_tile, tiles_dev)
    ringed = row_devices == 8 and col_devices == 4
    if ringed:
        quarter = local_rows // 4
        ring = functools.partial(lax.ppermute, axis_name="col", perm=list(NEXT.items()))
        spread = lax.all_to_all(
            panel.reshape(4, quarter, part),
            "row",
            split_axis=0,
            concat_axis=0,
            axis_index_groups=[[0, 2, 4, 6], [1, 3, 5, 7]],
            tiled=True,
        )
        first = ring(panel)
        spread, tiles = lax.optimization_barrier((spread, tiles))
        wanted = lax.all_to_all(spread, "col", split_axis=0, concat_axis=0, tiled=True)
        wanted, first, tiles = lax.optimization_barrier((wanted, first, tiles))
        second = ring(first)
        siblings = [(p, p ^ 1) for p in range(row_devices)]
        turns = [
            [(2 * c + m, 2 * step[c] + m) for c in range(4) for m in range(2)]
            for step in (NEXT, PREV)
        ]
        held = list(pair_factor(diag_inverse, wanted, quarter))
        pieces, plan = [], []
        for n in range(4):
            if n > 0:
                held = [lax.ppermute(x, "row", turn) for x, turn in zip(held, turns)]
            if n == 1:
                *held, second = lax.optimization_barrier((*held, second))
            for h, x in enumerate(held):
                steps = n if h == 0 else -n
                plan += [(h, steps, 0), (h, steps, 1)]
                pieces += [x, lax.ppermute(x, "row", siblings)]
        own = [panel, first, second, ring(second)]
    else:
        whole = lax.all_gather(panel, "col", axis=0)
        column = lax.all_gather(panel, "row", axis=0, tiled=True)
        column = column.reshape(col_devices, local_cols, part)
        partner = lax.all_to_all(column, "col", split_axis=0, concat_axis=0, tiled=True)
        pieces, plan = pair_factor(diag_inverse, partner, 768), [(0, 0, 0), (1, 0, 0)]
        own = [whole[s] for s in range(col_devices)]

    agg, landing = exchange_tiles(tiles, tiles_dev)
    entries, starts = order_tiles(
        landing, row_devices * CAP, tiles_dev, tile_cols, bm, bn, n_i, n_j
    )
    return front(
        place,
        entries,
        starts,
        diag_inverse,
        agg,
        trailing,
        own,
        list(range(4)),
        pieces,
        plan,
        ringed,
        bm,
        bn,
    )


def solution(mesh):
    in_specs = (
        P(),
        P("row", "col"),
        P("row", "col"),
        P("row", "col", None, None),
        P("row", "col", None, None),
        P("row", "col", None),
    )
    out_specs = (P("row", "col"), P("row", "col"))
    return jax.shard_map(
        per_device, mesh=mesh, in_specs=in_specs, out_specs=out_specs, check_vma=False
    )
```

```python
import functools

import jax
import jax.numpy as jnp
from jax import lax
from jax.experimental import pallas as pl
from jax.experimental.pallas import tpu as pltpu
from jax.sharding import PartitionSpec as P

TILE_ROWS = 8
TILE_COLS = 128
CAP = 2
VMEM_LIMIT = 58 << 20
NEXT = {0: 1, 1: 3, 3: 2, 2: 0}
PREV = {v: k for k, v in NEXT.items()}
NN = (((1,), (0,)), ((), ()))
NT = (((1,), (1,)), ((), ()))


def split(x):
    hi = x.astype(jnp.bfloat16)
    lo = (x - hi.astype(jnp.float32)).astype(jnp.bfloat16)
    return hi, lo


def ring_place(index, steps):
    at = (index ^ (index >> 1)) - steps & 3
    return at ^ (at >> 1)


def pair_kernel(d_ref, panel_ref, top_ref, low_ref):
    width = d_ref.shape[0]
    half = width // 2
    d_hi, d_lo = split(d_ref[...])
    hi, lo = split(jnp.concatenate([panel_ref[s] for s in range(4)], axis=1))
    for ref, rows, upto in ((top_ref, slice(0, half), half), (low_ref, slice(half, width), width)):
        d_rows = d_hi[rows, :upto]
        lhs = jnp.concatenate([d_rows, d_rows, d_lo[rows, :upto]], axis=1)
        rhs = jnp.concatenate([hi[:, :upto], lo[:, :upto], hi[:, :upto]], axis=1)
        ref[...] = lax.dot_general(lhs, rhs, NT, preferred_element_type=jnp.float32)


def pair_factor(d, panel, rows_step):
    width = d.shape[0]
    parts, rows, part = panel.shape
    out = jax.ShapeDtypeStruct((width // 2, rows), jnp.float32)
    out_block = pl.BlockSpec((width // 2, rows_step), lambda n: (0, n))
    return pl.pallas_call(
        pair_kernel,
        grid=(rows // rows_step,),
        out_shape=(out, out),
        in_specs=[
            pl.BlockSpec((width, width), lambda n: (0, 0)),
            pl.BlockSpec((parts, rows_step, part), lambda n: (0, n, 0)),
        ],
        out_specs=(out_block, out_block),
        compiler_params=pltpu.CompilerParams(vmem_limit_bytes=VMEM_LIMIT),
        cost_estimate=pl.CostEstimate(
            flops=6 * rows * width * width, bytes_accessed=8 * rows * width, transcendentals=0
        ),
        name="pair_factor",
    )(d, panel)


def front_kernel(
    ringed, own_plan, plan, place_ref, entry_ref, start_ref, d_ref, agg_ref, trail_ref, *refs
):
    n_own, n_pair = len(own_plan), len(plan)
    own_pieces, pieces = refs[:n_own], refs[n_own : n_own + n_pair]
    out_ref, block_ref = refs[n_own + n_pair : n_own + n_pair + 2]
    own_stage, stage, dt_left, dt_right, own_cat, pair_cat, full, sem = refs[n_own + n_pair + 2 :]
    j, i = pl.program_id(0), pl.program_id(1)
    n_i = pl.num_programs(1)
    bm, bn = out_ref.shape
    width = d_ref.shape[0]
    half = width // 2
    part = width // 4

    def own_copies():
        for n, s in enumerate(own_plan):
            source = ring_place(place_ref[1], s) if ringed else s
            lanes = pl.ds(pl.multiple_of(source * part, part), part)
            yield pltpu.make_async_copy(own_pieces[n], own_stage.at[:, lanes], sem.at[n])

    def pair_copies():
        for n, (upper, steps, swap) in enumerate(plan):
            depth, cols = pieces[n].shape
            block = 0
            if ringed:
                chip = ring_place(place_ref[0] // 2, steps)
                block = (place_ref[0] % 2 ^ swap) * 4 + chip
            at = pl.ds(pl.multiple_of(block * cols, TILE_COLS), cols)
            target = stage.at[pl.ds(upper * depth, depth), at]
            yield pltpu.make_async_copy(pieces[n], target, sem.at[n_own + n])

    @pl.when((i == 0) & (j == 0))
    def _():
        for c in own_copies():
            c.start()
        for c in pair_copies():
            c.start()
        hi, lo = split(d_ref[...].T)
        dt_left[...] = jnp.concatenate(
            [hi[:half, :half], hi[:half, :half], lo[:half, :half]], axis=0
        )
        dt_right[...] = jnp.concatenate([hi[:, half:], hi[:, half:], lo[:, half:]], axis=0)
        for c in own_copies():
            c.wait()

    rows = pl.ds(pl.multiple_of(i * bm, bm), bm)

    @pl.when(j == 0)
    def _():
        hi, lo = split(own_stage[rows, :])
        lhs = jnp.concatenate([hi[:, :half], lo[:, :half], hi[:, :half]], axis=1)
        full[:, :half] = lax.dot_general(
            lhs, dt_left[...], NN, preferred_element_type=jnp.float32
        )
        lhs = jnp.concatenate([hi, lo, hi], axis=1)
        full[:, half:] = lax.dot_general(
            lhs, dt_right[...], NN, preferred_element_type=jnp.float32
        )
        block_ref[...] = full[:, pl.ds(pl.multiple_of(place_ref[1] * part, part), part)]
        hi, lo = split(full[...])
        own_cat[rows, :] = jnp.concatenate([hi, hi, lo], axis=1)

    @pl.when((i == 0) & (j == 0))
    def _():
        for c in pair_copies():
            c.wait()

    @pl.when(i == 0)
    def _():
        cols = pl.ds(pl.multiple_of(j * bn, bn), bn)
        hi, lo = split(stage[:, cols])
        pair_cat[0:width, :] = hi
        pair_cat[width : 2 * width, :] = lo
        pair_cat[2 * width :, :] = hi

    for n in range(0, bn, 256):
        at = slice(n, n + 256)
        product = lax.dot_general(
            own_cat[rows, :], pair_cat[:, at], NN, preferred_element_type=jnp.float32
        )
        out_ref[:, at] = trail_ref[:, at] - product
    step = j * n_i + i

    def add(e, carry):
        r = pl.multiple_of(entry_ref[1, e], TILE_ROWS)
        c = pl.multiple_of(entry_ref[2, e], TILE_COLS)
        here = (pl.ds(r, TILE_ROWS), pl.ds(c, TILE_COLS))
        out_ref[here] = out_ref[here] + agg_ref[entry_ref[0, e]]
        return carry

    lax.fori_loop(start_ref[step], start_ref[step + 1], add, 0)


def front(place, entries, starts, d, agg, trailing, own, own_plan, pieces, plan, ringed, bm, bn):
    rows, cols = trailing.shape
    width = d.shape[0]
    half, part = width // 2, width // 4
    n_i = rows // bm
    whole = pl.BlockSpec(memory_space=pltpu.VMEM)
    smem = pl.BlockSpec(memory_space=pltpu.SMEM)
    block = pl.BlockSpec((bm, bn), lambda j, i: (i, j))
    operands = len(own) + len(pieces)
    return pl.pallas_call(
        functools.partial(front_kernel, ringed, own_plan, plan),
        grid=(cols // bn, n_i),
        out_shape=(
            jax.ShapeDtypeStruct((rows, cols), jnp.float32),
            jax.ShapeDtypeStruct((rows, part), jnp.float32),
        ),
        in_specs=[smem, smem, smem, whole, whole, block]
        + [pl.BlockSpec(memory_space=pl.ANY)] * operands,
        out_specs=(
            block,
            pl.BlockSpec((bm, part), lambda j, i: (jnp.where(j == 0, i, n_i - 1), 0)),
        ),
        scratch_shapes=[
            pltpu.VMEM((rows, width), jnp.float32),
            pltpu.VMEM((width, cols), jnp.float32),
            pltpu.VMEM((3 * half, half), jnp.bfloat16),
            pltpu.VMEM((3 * width, half), jnp.bfloat16),
            pltpu.VMEM((rows, 3 * width), jnp.bfloat16),
            pltpu.VMEM((3 * width, bn), jnp.bfloat16),
            pltpu.VMEM((bm, width), jnp.float32),
            pltpu.SemaphoreType.DMA((operands,)),
        ],
        compiler_params=pltpu.CompilerParams(vmem_limit_bytes=VMEM_LIMIT),
        cost_estimate=pl.CostEstimate(
            flops=6 * rows * width * (cols + width),
            bytes_accessed=8 * rows * cols + 4 * width * cols,
            transcendentals=0,
        ),
        name="front",
    )(place, entries, starts, d, agg, trailing, *own, *pieces)


def pack_tiles(agg_vals, agg_dest, agg_tile, tiles_dev):
    row_devices = lax.axis_size("row")
    agg = agg_vals.shape[2]
    targets = agg_dest.reshape(-1)
    tile_ids = agg_tile.reshape(-1)
    slots = row_devices * CAP
    order = jnp.arange(agg, dtype=jnp.int32)
    earlier = (targets[None, :] == targets[:, None]) & (order[None, :] < order[:, None])
    position = targets * CAP + jnp.sum(earlier.astype(jnp.int32), axis=1)
    hit = position[None, :] == jnp.arange(slots, dtype=jnp.int32)[:, None]
    send_ids = tiles_dev + jnp.sum(jnp.where(hit, tile_ids[None, :] - tiles_dev, 0), axis=1)
    values = agg_vals.reshape(agg, TILE_ROWS, TILE_COLS)
    send = jnp.zeros((slots, TILE_ROWS, TILE_COLS), jnp.float32).at[position].set(values)
    send = send.reshape(row_devices, CAP, TILE_ROWS, TILE_COLS)
    numbers = send_ids.astype(jnp.float32).reshape(row_devices, 1, 1, CAP)
    numbers = jnp.pad(numbers, ((0, 0), (0, 0), (0, TILE_ROWS - 1), (0, TILE_COLS - CAP)))
    return jnp.concatenate([send, numbers], axis=1)


def exchange_tiles(send, tiles_dev):
    got = lax.all_to_all(send, "row", split_axis=0, concat_axis=0, tiled=True)
    landing = got[:, CAP, 0, :CAP].astype(jnp.int32)
    landing = jnp.pad(landing, ((0, 0), (0, 1)), constant_values=tiles_dev)
    return got.reshape(-1, TILE_ROWS, TILE_COLS), landing.reshape(-1)


def order_tiles(landing, slots, tiles_dev, tile_cols, bm, bn, n_i, n_j):
    row = (landing // tile_cols) * TILE_ROWS
    col = (landing % tile_cols) * TILE_COLS
    count = landing.shape[0]
    number = jnp.arange(count, dtype=jnp.int32)
    step = jnp.where(landing < tiles_dev, (col // bn) * n_i + row // bm, n_i * n_j)
    key = step * count + number
    rank = jnp.sum((key[None, :] < key[:, None]).astype(jnp.int32), axis=1)
    hit = (rank[None, :] == jnp.arange(slots, dtype=jnp.int32)[:, None]).astype(jnp.int32)
    fields = jnp.stack([number, row % bm, col % bn])
    entries = jnp.sum(hit[None] * fields[:, None, :], axis=2)
    edges = jnp.arange(n_i * n_j + 1, dtype=jnp.int32)
    starts = jnp.sum((step[None, :] < edges[:, None]).astype(jnp.int32), axis=1)
    return entries, starts


def per_device(diag_inverse, panel, trailing, agg_vals, agg_dest, agg_tile):
    row_devices = lax.axis_size("row")
    col_devices = lax.axis_size("col")
    local_rows, local_cols = trailing.shape
    part = panel.shape[1]
    col_index = lax.axis_index("col")
    tile_cols = local_cols // TILE_COLS
    tiles_dev = (local_rows // TILE_ROWS) * tile_cols
    bm = 768 if local_rows % 768 == 0 else local_rows
    bn = 1024
    n_i, n_j = local_rows // bm, local_cols // bn

    row_index = lax.axis_index("row")
    place = jnp.stack([row_index, col_index]).astype(jnp.int32)
    tiles = pack_tiles(agg_vals, agg_dest, agg_tile, tiles_dev)
    ringed = row_devices == 8 and col_devices == 4
    if ringed:
        quarter = local_rows // 4
        ring = functools.partial(lax.ppermute, axis_name="col", perm=list(NEXT.items()))
        spread = lax.all_to_all(
            panel.reshape(4, quarter, part),
            "row",
            split_axis=0,
            concat_axis=0,
            axis_index_groups=[[0, 2, 4, 6], [1, 3, 5, 7]],
            tiled=True,
        )
        spread, first, tiles = lax.optimization_barrier((spread, ring(panel), tiles))
        wanted = lax.all_to_all(spread, "col", split_axis=0, concat_axis=0, tiled=True)
        wanted, first, tiles = lax.optimization_barrier((wanted, first, tiles))
        second = ring(first)
        siblings = [(p, p ^ 1) for p in range(row_devices)]
        turns = [
            [(2 * c + m, 2 * step[c] + m) for c in range(4) for m in range(2)]
            for step in (NEXT, PREV)
        ]
        held = list(pair_factor(diag_inverse, wanted, quarter))
        pieces, plan = [], []
        for n in range(4):
            if n > 0:
                held = [lax.ppermute(x, "row", turn) for x, turn in zip(held, turns)]
            if n == 1:
                *held, second = lax.optimization_barrier((*held, second))
            for h, x in enumerate(held):
                steps = n if h == 0 else -n
                plan += [(h, steps, 0), (h, steps, 1)]
                pieces += [x, lax.ppermute(x, "row", siblings)]
        own = [panel, first, second, ring(second)]
    else:
        whole = lax.all_gather(panel, "col", axis=0)
        column = lax.all_gather(panel, "row", axis=0, tiled=True)
        column = column.reshape(col_devices, local_cols, part)
        partner = lax.all_to_all(column, "col", split_axis=0, concat_axis=0, tiled=True)
        pieces, plan = pair_factor(diag_inverse, partner, 768), [(0, 0, 0), (1, 0, 0)]
        own = [whole[s] for s in range(col_devices)]

    agg, landing = exchange_tiles(tiles, tiles_dev)
    entries, starts = order_tiles(
        landing, row_devices * CAP, tiles_dev, tile_cols, bm, bn, n_i, n_j
    )
    return front(
        place,
        entries,
        starts,
        diag_inverse,
        agg,
        trailing,
        own,
        list(range(4)),
        pieces,
        plan,
        ringed,
        bm,
        bn,
    )


def solution(mesh):
    in_specs = (
        P(),
        P("row", "col"),
        P("row", "col"),
        P("row", "col", None, None),
        P("row", "col", None, None),
        P("row", "col", None),
    )
    out_specs = (P("row", "col"), P("row", "col"))
    return jax.shard_map(
        per_device, mesh=mesh, in_specs=in_specs, out_specs=out_specs, check_vma=False
    )
```

```python
import functools

import jax
import jax.numpy as jnp
from jax import lax
from jax.experimental import pallas as pl
from jax.experimental.pallas import tpu as pltpu
from jax.sharding import PartitionSpec as P

TILE_ROWS = 8
TILE_COLS = 128
CAP = 2
VMEM_LIMIT = 58 << 20
NEXT = {0: 1, 1: 3, 3: 2, 2: 0}
PREV = {v: k for k, v in NEXT.items()}
NN = (((1,), (0,)), ((), ()))
NT = (((1,), (1,)), ((), ()))


def split(x):
    hi = x.astype(jnp.bfloat16)
    lo = (x - hi.astype(jnp.float32)).astype(jnp.bfloat16)
    return hi, lo


def ring_place(index, steps):
    at = (index ^ (index >> 1)) - steps & 3
    return at ^ (at >> 1)


def pair_kernel(d_ref, panel_ref, top_ref, low_ref):
    width = d_ref.shape[0]
    half = width // 2
    d_hi, d_lo = split(d_ref[...])
    hi, lo = split(jnp.concatenate([panel_ref[s] for s in range(4)], axis=1))
    for ref, rows, upto in ((top_ref, slice(0, half), half), (low_ref, slice(half, width), width)):
        d_rows = d_hi[rows, :upto]
        lhs = jnp.concatenate([d_rows, d_rows, d_lo[rows, :upto]], axis=1)
        rhs = jnp.concatenate([hi[:, :upto], lo[:, :upto], hi[:, :upto]], axis=1)
        ref[...] = lax.dot_general(lhs, rhs, NT, preferred_element_type=jnp.float32)


def pair_factor(d, panel, rows_step):
    width = d.shape[0]
    parts, rows, part = panel.shape
    out = jax.ShapeDtypeStruct((width // 2, rows), jnp.float32)
    out_block = pl.BlockSpec((width // 2, rows_step), lambda n: (0, n))
    return pl.pallas_call(
        pair_kernel,
        grid=(rows // rows_step,),
        out_shape=(out, out),
        in_specs=[
            pl.BlockSpec((width, width), lambda n: (0, 0)),
            pl.BlockSpec((parts, rows_step, part), lambda n: (0, n, 0)),
        ],
        out_specs=(out_block, out_block),
        compiler_params=pltpu.CompilerParams(vmem_limit_bytes=VMEM_LIMIT),
        cost_estimate=pl.CostEstimate(
            flops=6 * rows * width * width, bytes_accessed=8 * rows * width, transcendentals=0
        ),
        name="pair_factor",
    )(d, panel)


def front_kernel(
    ringed, own_plan, plan, place_ref, entry_ref, start_ref, d_ref, agg_ref, trail_ref, *refs
):
    n_own, n_pair = len(own_plan), len(plan)
    own_pieces, pieces = refs[:n_own], refs[n_own : n_own + n_pair]
    out_ref, block_ref = refs[n_own + n_pair : n_own + n_pair + 2]
    own_stage, stage, dt_left, dt_right, own_cat, pair_cat, full, sem = refs[n_own + n_pair + 2 :]
    j, i = pl.program_id(0), pl.program_id(1)
    n_i = pl.num_programs(1)
    bm, bn = out_ref.shape
    width = d_ref.shape[0]
    half = width // 2
    part = width // 4

    def own_copies():
        for n, (s, row) in enumerate(own_plan):
            source = ring_place(place_ref[1], s) if ringed else s
            lanes = pl.ds(pl.multiple_of(source * part, part), part)
            target = own_stage.at[pl.ds(row, own_pieces[n].shape[0]), lanes]
            yield pltpu.make_async_copy(own_pieces[n], target, sem.at[n])

    def pair_copies():
        for n, (upper, steps, swap) in enumerate(plan):
            depth, cols = pieces[n].shape
            block = 0
            if ringed:
                chip = ring_place(place_ref[0] // 2, steps)
                block = (place_ref[0] % 2 ^ swap) * 4 + chip
            at = pl.ds(pl.multiple_of(block * cols, TILE_COLS), cols)
            target = stage.at[pl.ds(upper * depth, depth), at]
            yield pltpu.make_async_copy(pieces[n], target, sem.at[n_own + n])

    @pl.when((i == 0) & (j == 0))
    def _():
        for c in own_copies():
            c.start()
        for c in pair_copies():
            c.start()
        hi, lo = split(d_ref[...].T)
        dt_left[...] = jnp.concatenate(
            [hi[:half, :half], hi[:half, :half], lo[:half, :half]], axis=0
        )
        dt_right[...] = jnp.concatenate([hi[:, half:], hi[:, half:], lo[:, half:]], axis=0)
        for c in own_copies():
            c.wait()

    rows = pl.ds(pl.multiple_of(i * bm, bm), bm)

    @pl.when(j == 0)
    def _():
        hi, lo = split(own_stage[rows, :])
        lhs = jnp.concatenate([hi[:, :half], lo[:, :half], hi[:, :half]], axis=1)
        full[:, :half] = lax.dot_general(
            lhs, dt_left[...], NN, preferred_element_type=jnp.float32
        )
        lhs = jnp.concatenate([hi, lo, hi], axis=1)
        full[:, half:] = lax.dot_general(
            lhs, dt_right[...], NN, preferred_element_type=jnp.float32
        )
        block_ref[...] = full[:, pl.ds(pl.multiple_of(place_ref[1] * part, part), part)]
        hi, lo = split(full[...])
        own_cat[rows, :] = jnp.concatenate([hi, hi, lo], axis=1)

    @pl.when((i == 0) & (j == 0))
    def _():
        for c in pair_copies():
            c.wait()

    @pl.when(i == 0)
    def _():
        cols = pl.ds(pl.multiple_of(j * bn, bn), bn)
        hi, lo = split(stage[:, cols])
        pair_cat[0:width, :] = hi
        pair_cat[width : 2 * width, :] = lo
        pair_cat[2 * width :, :] = hi

    for n in range(0, bn, 256):
        at = slice(n, n + 256)
        product = lax.dot_general(
            own_cat[rows, :], pair_cat[:, at], NN, preferred_element_type=jnp.float32
        )
        out_ref[:, at] = trail_ref[:, at] - product
    step = j * n_i + i

    def add(e, carry):
        r = pl.multiple_of(entry_ref[1, e], TILE_ROWS)
        c = pl.multiple_of(entry_ref[2, e], TILE_COLS)
        here = (pl.ds(r, TILE_ROWS), pl.ds(c, TILE_COLS))
        out_ref[here] = out_ref[here] + agg_ref[entry_ref[0, e]]
        return carry

    lax.fori_loop(start_ref[step], start_ref[step + 1], add, 0)


def front(place, entries, starts, d, agg, trailing, own, own_plan, pieces, plan, ringed, bm, bn):
    rows, cols = trailing.shape
    width = d.shape[0]
    half, part = width // 2, width // 4
    n_i = rows // bm
    whole = pl.BlockSpec(memory_space=pltpu.VMEM)
    smem = pl.BlockSpec(memory_space=pltpu.SMEM)
    block = pl.BlockSpec((bm, bn), lambda j, i: (i, j))
    operands = len(own) + len(pieces)
    return pl.pallas_call(
        functools.partial(front_kernel, ringed, own_plan, plan),
        grid=(cols // bn, n_i),
        out_shape=(
            jax.ShapeDtypeStruct((rows, cols), jnp.float32),
            jax.ShapeDtypeStruct((rows, part), jnp.float32),
        ),
        in_specs=[smem, smem, smem, whole, whole, block]
        + [pl.BlockSpec(memory_space=pl.ANY)] * operands,
        out_specs=(
            block,
            pl.BlockSpec((bm, part), lambda j, i: (jnp.where(j == 0, i, n_i - 1), 0)),
        ),
        scratch_shapes=[
            pltpu.VMEM((rows, width), jnp.float32),
            pltpu.VMEM((width, cols), jnp.float32),
            pltpu.VMEM((3 * half, half), jnp.bfloat16),
            pltpu.VMEM((3 * width, half), jnp.bfloat16),
            pltpu.VMEM((rows, 3 * width), jnp.bfloat16),
            pltpu.VMEM((3 * width, bn), jnp.bfloat16),
            pltpu.VMEM((bm, width), jnp.float32),
            pltpu.SemaphoreType.DMA((operands,)),
        ],
        compiler_params=pltpu.CompilerParams(vmem_limit_bytes=VMEM_LIMIT),
        cost_estimate=pl.CostEstimate(
            flops=6 * rows * width * (cols + width),
            bytes_accessed=8 * rows * cols + 4 * width * cols,
            transcendentals=0,
        ),
        name="front",
    )(place, entries, starts, d, agg, trailing, *own, *pieces)


def pack_tiles(agg_vals, agg_dest, agg_tile, tiles_dev):
    row_devices = lax.axis_size("row")
    agg = agg_vals.shape[2]
    targets = agg_dest.reshape(-1)
    tile_ids = agg_tile.reshape(-1)
    slots = row_devices * CAP
    order = jnp.arange(agg, dtype=jnp.int32)
    earlier = (targets[None, :] == targets[:, None]) & (order[None, :] < order[:, None])
    position = targets * CAP + jnp.sum(earlier.astype(jnp.int32), axis=1)
    hit = position[None, :] == jnp.arange(slots, dtype=jnp.int32)[:, None]
    send_ids = tiles_dev + jnp.sum(jnp.where(hit, tile_ids[None, :] - tiles_dev, 0), axis=1)
    values = agg_vals.reshape(agg, TILE_ROWS, TILE_COLS)
    send = jnp.zeros((slots, TILE_ROWS, TILE_COLS), jnp.float32).at[position].set(values)
    send = send.reshape(row_devices, CAP, TILE_ROWS, TILE_COLS)
    numbers = send_ids.astype(jnp.float32).reshape(row_devices, 1, 1, CAP)
    numbers = jnp.pad(numbers, ((0, 0), (0, 0), (0, TILE_ROWS - 1), (0, TILE_COLS - CAP)))
    return jnp.concatenate([send, numbers], axis=1)


def exchange_tiles(send, tiles_dev):
    got = lax.all_to_all(send, "row", split_axis=0, concat_axis=0, tiled=True)
    landing = got[:, CAP, 0, :CAP].astype(jnp.int32)
    landing = jnp.pad(landing, ((0, 0), (0, 1)), constant_values=tiles_dev)
    return got.reshape(-1, TILE_ROWS, TILE_COLS), landing.reshape(-1)


def order_tiles(landing, slots, tiles_dev, tile_cols, bm, bn, n_i, n_j):
    row = (landing // tile_cols) * TILE_ROWS
    col = (landing % tile_cols) * TILE_COLS
    count = landing.shape[0]
    number = jnp.arange(count, dtype=jnp.int32)
    step = jnp.where(landing < tiles_dev, (col // bn) * n_i + row // bm, n_i * n_j)
    key = step * count + number
    rank = jnp.sum((key[None, :] < key[:, None]).astype(jnp.int32), axis=1)
    hit = (rank[None, :] == jnp.arange(slots, dtype=jnp.int32)[:, None]).astype(jnp.int32)
    fields = jnp.stack([number, row % bm, col % bn])
    entries = jnp.sum(hit[None] * fields[:, None, :], axis=2)
    edges = jnp.arange(n_i * n_j + 1, dtype=jnp.int32)
    starts = jnp.sum((step[None, :] < edges[:, None]).astype(jnp.int32), axis=1)
    return entries, starts


def per_device(diag_inverse, panel, trailing, agg_vals, agg_dest, agg_tile):
    row_devices = lax.axis_size("row")
    col_devices = lax.axis_size("col")
    local_rows, local_cols = trailing.shape
    part = panel.shape[1]
    col_index = lax.axis_index("col")
    tile_cols = local_cols // TILE_COLS
    tiles_dev = (local_rows // TILE_ROWS) * tile_cols
    bm, bn = local_rows, 512
    n_i, n_j = local_rows // bm, local_cols // bn

    row_index = lax.axis_index("row")
    place = jnp.stack([row_index, col_index]).astype(jnp.int32)
    tiles = pack_tiles(agg_vals, agg_dest, agg_tile, tiles_dev)
    ringed = row_devices == 8 and col_devices == 4
    if ringed:
        quarter = local_rows // 4
        ring = functools.partial(lax.ppermute, axis_name="col", perm=list(NEXT.items()))
        spread = lax.all_to_all(
            panel.reshape(4, quarter, part),
            "row",
            split_axis=0,
            concat_axis=0,
            axis_index_groups=[[0, 2, 4, 6], [1, 3, 5, 7]],
            tiled=True,
        )
        first = ring(panel)
        half = local_rows // 2
        spread, upper, lower, tiles = lax.optimization_barrier(
            (spread, first[:half], first[half:], tiles)
        )
        wanted = lax.all_to_all(spread, "col", split_axis=0, concat_axis=0, tiled=True)
        wanted, upper, lower, tiles = lax.optimization_barrier((wanted, upper, lower, tiles))
        second = [ring(upper), ring(lower)]
        third = [ring(x) for x in second]
        siblings = [(p, p ^ 1) for p in range(row_devices)]
        turns = [
            [(2 * c + m, 2 * step[c] + m) for c in range(4) for m in range(2)]
            for step in (NEXT, PREV)
        ]
        held = list(pair_factor(diag_inverse, wanted, quarter))
        pieces, plan = [], []
        for n in range(4):
            if n > 0:
                held = [lax.ppermute(x, "row", turn) for x, turn in zip(held, turns)]
            if n == 1:
                *held, second[0], second[1] = lax.optimization_barrier((*held, *second))
            if n == 2:
                *held, third[0] = lax.optimization_barrier((*held, third[0]))
            for h, x in enumerate(held):
                steps = n if h == 0 else -n
                plan += [(h, steps, 0), (h, steps, 1)]
                pieces += [x, lax.ppermute(x, "row", siblings)]
        own = [panel, first, *second, *third]
        own_plan = [(0, 0), (1, 0), (2, 0), (2, half), (3, 0), (3, half)]
    else:
        whole = lax.all_gather(panel, "col", axis=0)
        column = lax.all_gather(panel, "row", axis=0, tiled=True)
        column = column.reshape(col_devices, local_cols, part)
        partner = lax.all_to_all(column, "col", split_axis=0, concat_axis=0, tiled=True)
        pieces, plan = pair_factor(diag_inverse, partner, 768), [(0, 0, 0), (1, 0, 0)]
        own = [whole[s] for s in range(col_devices)]
        own_plan = [(s, 0) for s in range(col_devices)]

    agg, landing = exchange_tiles(tiles, tiles_dev)
    entries, starts = order_tiles(
        landing, row_devices * CAP, tiles_dev, tile_cols, bm, bn, n_i, n_j
    )
    return front(
        place,
        entries,
        starts,
        diag_inverse,
        agg,
        trailing,
        own,
        own_plan,
        pieces,
        plan,
        ringed,
        bm,
        bn,
    )


def solution(mesh):
    in_specs = (
        P(),
        P("row", "col"),
        P("row", "col"),
        P("row", "col", None, None),
        P("row", "col", None, None),
        P("row", "col", None),
    )
    out_specs = (P("row", "col"), P("row", "col"))
    return jax.shard_map(
        per_device, mesh=mesh, in_specs=in_specs, out_specs=out_specs, check_vma=False
    )
```

```python
import functools

import jax
import jax.numpy as jnp
from jax import lax
from jax.experimental import pallas as pl
from jax.experimental.pallas import tpu as pltpu
from jax.sharding import PartitionSpec as P

TILE_ROWS = 8
TILE_COLS = 128
CAP = 2
VMEM_LIMIT = 58 << 20
NEXT = {0: 1, 1: 3, 3: 2, 2: 0}
PREV = {v: k for k, v in NEXT.items()}
NN = (((1,), (0,)), ((), ()))
NT = (((1,), (1,)), ((), ()))


def split(x):
    hi = x.astype(jnp.bfloat16)
    lo = (x - hi.astype(jnp.float32)).astype(jnp.bfloat16)
    return hi, lo


def ring_place(index, steps):
    at = (index ^ (index >> 1)) - steps & 3
    return at ^ (at >> 1)


def pair_kernel(d_ref, panel_ref, top_ref, low_ref):
    width = d_ref.shape[0]
    half = width // 2
    d_hi, d_lo = split(d_ref[...])
    hi, lo = split(jnp.concatenate([panel_ref[s] for s in range(4)], axis=1))
    for ref, rows, upto in ((top_ref, slice(0, half), half), (low_ref, slice(half, width), width)):
        d_rows = d_hi[rows, :upto]
        lhs = jnp.concatenate([d_rows, d_rows, d_lo[rows, :upto]], axis=1)
        rhs = jnp.concatenate([hi[:, :upto], lo[:, :upto], hi[:, :upto]], axis=1)
        ref[...] = lax.dot_general(lhs, rhs, NT, preferred_element_type=jnp.float32)


def pair_factor(d, panel, rows_step):
    width = d.shape[0]
    parts, rows, part = panel.shape
    out = jax.ShapeDtypeStruct((width // 2, rows), jnp.float32)
    out_block = pl.BlockSpec((width // 2, rows_step), lambda n: (0, n))
    return pl.pallas_call(
        pair_kernel,
        grid=(rows // rows_step,),
        out_shape=(out, out),
        in_specs=[
            pl.BlockSpec((width, width), lambda n: (0, 0)),
            pl.BlockSpec((parts, rows_step, part), lambda n: (0, n, 0)),
        ],
        out_specs=(out_block, out_block),
        compiler_params=pltpu.CompilerParams(vmem_limit_bytes=VMEM_LIMIT),
        cost_estimate=pl.CostEstimate(
            flops=6 * rows * width * width, bytes_accessed=8 * rows * width, transcendentals=0
        ),
        name="pair_factor",
    )(d, panel)


def front_kernel(
    ringed, own_plan, plan, place_ref, entry_ref, start_ref, d_ref, agg_ref, trail_ref, *refs
):
    n_own, n_pair = len(own_plan), len(plan)
    own_pieces, pieces = refs[:n_own], refs[n_own : n_own + n_pair]
    out_ref, block_ref = refs[n_own + n_pair : n_own + n_pair + 2]
    own_stage, stage, dt_left, dt_right, own_cat, pair_cat, full, sem = refs[n_own + n_pair + 2 :]
    j, i = pl.program_id(0), pl.program_id(1)
    n_i = pl.num_programs(1)
    bm, bn = out_ref.shape
    width = d_ref.shape[0]
    half = width // 2
    part = width // 4

    def own_copies():
        for n, s in enumerate(own_plan):
            source = ring_place(place_ref[1], s) if ringed else s
            lanes = pl.ds(pl.multiple_of(source * part, part), part)
            yield pltpu.make_async_copy(own_pieces[n], own_stage.at[:, lanes], sem.at[n])

    def pair_copies():
        for n, (upper, steps, swap) in enumerate(plan):
            depth, cols = pieces[n].shape
            block = 0
            if ringed:
                chip = ring_place(place_ref[0] // 2, steps)
                block = (place_ref[0] % 2 ^ swap) * 4 + chip
            at = pl.ds(pl.multiple_of(block * cols, TILE_COLS), cols)
            target = stage.at[pl.ds(upper * depth, depth), at]
            yield pltpu.make_async_copy(pieces[n], target, sem.at[n_own + n])

    @pl.when((i == 0) & (j == 0))
    def _():
        for c in own_copies():
            c.start()
        for c in pair_copies():
            c.start()
        hi, lo = split(d_ref[...].T)
        dt_left[...] = jnp.concatenate(
            [hi[:half, :half], hi[:half, :half], lo[:half, :half]], axis=0
        )
        dt_right[...] = jnp.concatenate([hi[:, half:], hi[:, half:], lo[:, half:]], axis=0)
        for c in own_copies():
            c.wait()

    rows = pl.ds(pl.multiple_of(i * bm, bm), bm)

    @pl.when(j == 0)
    def _():
        hi, lo = split(own_stage[rows, :])
        lhs = jnp.concatenate([hi[:, :half], lo[:, :half], hi[:, :half]], axis=1)
        full[:, :half] = lax.dot_general(
            lhs, dt_left[...], NN, preferred_element_type=jnp.float32
        )
        lhs = jnp.concatenate([hi, lo, hi], axis=1)
        full[:, half:] = lax.dot_general(
            lhs, dt_right[...], NN, preferred_element_type=jnp.float32
        )
        block_ref[...] = full[:, pl.ds(pl.multiple_of(place_ref[1] * part, part), part)]
        hi, lo = split(full[...])
        own_cat[rows, :] = jnp.concatenate([hi, hi, lo], axis=1)

    @pl.when((i == 0) & (j == 0))
    def _():
        for c in pair_copies():
            c.wait()

    @pl.when(i == 0)
    def _():
        cols = pl.ds(pl.multiple_of(j * bn, bn), bn)
        hi, lo = split(stage[:, cols])
        pair_cat[0:width, :] = hi
        pair_cat[width : 2 * width, :] = lo
        pair_cat[2 * width :, :] = hi

    for n in range(0, bn, 256):
        at = slice(n, n + 256)
        product = lax.dot_general(
            own_cat[rows, :], pair_cat[:, at], NN, preferred_element_type=jnp.float32
        )
        out_ref[:, at] = trail_ref[:, at] - product
    step = j * n_i + i

    def add(e, carry):
        r = pl.multiple_of(entry_ref[1, e], TILE_ROWS)
        c = pl.multiple_of(entry_ref[2, e], TILE_COLS)
        here = (pl.ds(r, TILE_ROWS), pl.ds(c, TILE_COLS))
        out_ref[here] = out_ref[here] + agg_ref[entry_ref[0, e]]
        return carry

    lax.fori_loop(start_ref[step], start_ref[step + 1], add, 0)


def front(place, entries, starts, d, agg, trailing, own, own_plan, pieces, plan, ringed, bm, bn):
    rows, cols = trailing.shape
    width = d.shape[0]
    half, part = width // 2, width // 4
    n_i = rows // bm
    whole = pl.BlockSpec(memory_space=pltpu.VMEM)
    smem = pl.BlockSpec(memory_space=pltpu.SMEM)
    block = pl.BlockSpec((bm, bn), lambda j, i: (i, j))
    operands = len(own) + len(pieces)
    return pl.pallas_call(
        functools.partial(front_kernel, ringed, own_plan, plan),
        grid=(cols // bn, n_i),
        out_shape=(
            jax.ShapeDtypeStruct((rows, cols), jnp.float32),
            jax.ShapeDtypeStruct((rows, part), jnp.float32),
        ),
        in_specs=[smem, smem, smem, whole, whole, block]
        + [pl.BlockSpec(memory_space=pl.ANY)] * operands,
        out_specs=(
            block,
            pl.BlockSpec((bm, part), lambda j, i: (jnp.where(j == 0, i, n_i - 1), 0)),
        ),
        scratch_shapes=[
            pltpu.VMEM((rows, width), jnp.float32),
            pltpu.VMEM((width, cols), jnp.float32),
            pltpu.VMEM((3 * half, half), jnp.bfloat16),
            pltpu.VMEM((3 * width, half), jnp.bfloat16),
            pltpu.VMEM((rows, 3 * width), jnp.bfloat16),
            pltpu.VMEM((3 * width, bn), jnp.bfloat16),
            pltpu.VMEM((bm, width), jnp.float32),
            pltpu.SemaphoreType.DMA((operands,)),
        ],
        compiler_params=pltpu.CompilerParams(vmem_limit_bytes=VMEM_LIMIT),
        cost_estimate=pl.CostEstimate(
            flops=6 * rows * width * (cols + width),
            bytes_accessed=8 * rows * cols + 4 * width * cols,
            transcendentals=0,
        ),
        name="front",
    )(place, entries, starts, d, agg, trailing, *own, *pieces)


def pack_tiles(agg_vals, agg_dest, agg_tile, tiles_dev):
    row_devices = lax.axis_size("row")
    agg = agg_vals.shape[2]
    targets = agg_dest.reshape(-1)
    tile_ids = agg_tile.reshape(-1)
    slots = row_devices * CAP
    order = jnp.arange(agg, dtype=jnp.int32)
    earlier = (targets[None, :] == targets[:, None]) & (order[None, :] < order[:, None])
    position = targets * CAP + jnp.sum(earlier.astype(jnp.int32), axis=1)
    hit = position[None, :] == jnp.arange(slots, dtype=jnp.int32)[:, None]
    send_ids = tiles_dev + jnp.sum(jnp.where(hit, tile_ids[None, :] - tiles_dev, 0), axis=1)
    values = agg_vals.reshape(agg, TILE_ROWS, TILE_COLS)
    send = jnp.zeros((slots, TILE_ROWS, TILE_COLS), jnp.float32).at[position].set(values)
    send = send.reshape(row_devices, CAP, TILE_ROWS, TILE_COLS)
    numbers = send_ids.astype(jnp.float32).reshape(row_devices, 1, 1, CAP)
    numbers = jnp.pad(numbers, ((0, 0), (0, 0), (0, TILE_ROWS - 1), (0, TILE_COLS - CAP)))
    return jnp.concatenate([send, numbers], axis=1)


def exchange_tiles(send, tiles_dev):
    got = lax.all_to_all(send, "row", split_axis=0, concat_axis=0, tiled=True)
    landing = got[:, CAP, 0, :CAP].astype(jnp.int32)
    landing = jnp.pad(landing, ((0, 0), (0, 1)), constant_values=tiles_dev)
    return got.reshape(-1, TILE_ROWS, TILE_COLS), landing.reshape(-1)


def order_tiles(landing, slots, tiles_dev, tile_cols, bm, bn, n_i, n_j):
    row = (landing // tile_cols) * TILE_ROWS
    col = (landing % tile_cols) * TILE_COLS
    count = landing.shape[0]
    number = jnp.arange(count, dtype=jnp.int32)
    step = jnp.where(landing < tiles_dev, (col // bn) * n_i + row // bm, n_i * n_j)
    key = step * count + number
    rank = jnp.sum((key[None, :] < key[:, None]).astype(jnp.int32), axis=1)
    hit = (rank[None, :] == jnp.arange(slots, dtype=jnp.int32)[:, None]).astype(jnp.int32)
    fields = jnp.stack([number, row % bm, col % bn])
    entries = jnp.sum(hit[None] * fields[:, None, :], axis=2)
    edges = jnp.arange(n_i * n_j + 1, dtype=jnp.int32)
    starts = jnp.sum((step[None, :] < edges[:, None]).astype(jnp.int32), axis=1)
    return entries, starts


def per_device(diag_inverse, panel, trailing, agg_vals, agg_dest, agg_tile):
    row_devices = lax.axis_size("row")
    col_devices = lax.axis_size("col")
    local_rows, local_cols = trailing.shape
    part = panel.shape[1]
    col_index = lax.axis_index("col")
    tile_cols = local_cols // TILE_COLS
    tiles_dev = (local_rows // TILE_ROWS) * tile_cols
    bm, bn = local_rows, 512
    n_i, n_j = local_rows // bm, local_cols // bn

    row_index = lax.axis_index("row")
    place = jnp.stack([row_index, col_index]).astype(jnp.int32)
    tiles = pack_tiles(agg_vals, agg_dest, agg_tile, tiles_dev)
    ringed = row_devices == 8 and col_devices == 4
    if ringed:
        quarter = local_rows // 4
        ring = functools.partial(lax.ppermute, axis_name="col", perm=list(NEXT.items()))
        spread = lax.all_to_all(
            panel.reshape(4, quarter, part),
            "row",
            split_axis=0,
            concat_axis=0,
            axis_index_groups=[[0, 2, 4, 6], [1, 3, 5, 7]],
            tiled=True,
        )
        spread, first, tiles = lax.optimization_barrier((spread, ring(panel), tiles))
        wanted = lax.all_to_all(spread, "col", split_axis=0, concat_axis=0, tiled=True)
        wanted, first, mine, tiles = lax.optimization_barrier((wanted, first, panel, tiles))
        third = lax.ppermute(mine, "col", list(PREV.items()))
        second = ring(first)
        siblings = [(p, p ^ 1) for p in range(row_devices)]
        turns = [
            [(2 * c + m, 2 * step[c] + m) for c in range(4) for m in range(2)]
            for step in (NEXT, PREV)
        ]
        held = list(pair_factor(diag_inverse, wanted, quarter))
        pieces, plan = [], []
        for n in range(4):
            if n > 0:
                held = [lax.ppermute(x, "row", turn) for x, turn in zip(held, turns)]
            if n == 1:
                *held, third = lax.optimization_barrier((*held, third))
            for h, x in enumerate(held):
                steps = n if h == 0 else -n
                plan += [(h, steps, 0), (h, steps, 1)]
                pieces += [x, lax.ppermute(x, "row", siblings)]
        own = [panel, first, second, third]
    else:
        whole = lax.all_gather(panel, "col", axis=0)
        column = lax.all_gather(panel, "row", axis=0, tiled=True)
        column = column.reshape(col_devices, local_cols, part)
        partner = lax.all_to_all(column, "col", split_axis=0, concat_axis=0, tiled=True)
        pieces, plan = pair_factor(diag_inverse, partner, 768), [(0, 0, 0), (1, 0, 0)]
        own = [whole[s] for s in range(col_devices)]

    agg, landing = exchange_tiles(tiles, tiles_dev)
    entries, starts = order_tiles(
        landing, row_devices * CAP, tiles_dev, tile_cols, bm, bn, n_i, n_j
    )
    return front(
        place,
        entries,
        starts,
        diag_inverse,
        agg,
        trailing,
        own,
        list(range(4)),
        pieces,
        plan,
        ringed,
        bm,
        bn,
    )


def solution(mesh):
    in_specs = (
        P(),
        P("row", "col"),
        P("row", "col"),
        P("row", "col", None, None),
        P("row", "col", None, None),
        P("row", "col", None),
    )
    out_specs = (P("row", "col"), P("row", "col"))
    return jax.shard_map(
        per_device, mesh=mesh, in_specs=in_specs, out_specs=out_specs, check_vma=False
    )
```

```python
import functools

import jax
import jax.numpy as jnp
from jax import lax
from jax.experimental import pallas as pl
from jax.experimental.pallas import tpu as pltpu
from jax.sharding import PartitionSpec as P

TILE_ROWS = 8
TILE_COLS = 128
CAP = 2
VMEM_LIMIT = 58 << 20
NEXT = {0: 1, 1: 3, 3: 2, 2: 0}
PREV = {v: k for k, v in NEXT.items()}
NN = (((1,), (0,)), ((), ()))
NT = (((1,), (1,)), ((), ()))


def split(x):
    hi = x.astype(jnp.bfloat16)
    lo = (x - hi.astype(jnp.float32)).astype(jnp.bfloat16)
    return hi, lo


def ring_place(index, steps):
    at = (index ^ (index >> 1)) - steps & 3
    return at ^ (at >> 1)


def pair_kernel(d_ref, panel_ref, top_ref, low_ref):
    width = d_ref.shape[0]
    half = width // 2
    d_hi, d_lo = split(d_ref[...])
    hi, lo = split(jnp.concatenate([panel_ref[s] for s in range(4)], axis=1))
    for ref, rows, upto in ((top_ref, slice(0, half), half), (low_ref, slice(half, width), width)):
        d_rows = d_hi[rows, :upto]
        lhs = jnp.concatenate([d_rows, d_rows, d_lo[rows, :upto]], axis=1)
        rhs = jnp.concatenate([hi[:, :upto], lo[:, :upto], hi[:, :upto]], axis=1)
        ref[...] = lax.dot_general(lhs, rhs, NT, preferred_element_type=jnp.float32)


def pair_factor(d, panel, rows_step):
    width = d.shape[0]
    parts, rows, part = panel.shape
    out = jax.ShapeDtypeStruct((width // 2, rows), jnp.float32)
    out_block = pl.BlockSpec((width // 2, rows_step), lambda n: (0, n))
    return pl.pallas_call(
        pair_kernel,
        grid=(rows // rows_step,),
        out_shape=(out, out),
        in_specs=[
            pl.BlockSpec((width, width), lambda n: (0, 0)),
            pl.BlockSpec((parts, rows_step, part), lambda n: (0, n, 0)),
        ],
        out_specs=(out_block, out_block),
        compiler_params=pltpu.CompilerParams(vmem_limit_bytes=VMEM_LIMIT),
        cost_estimate=pl.CostEstimate(
            flops=6 * rows * width * width, bytes_accessed=8 * rows * width, transcendentals=0
        ),
        name="pair_factor",
    )(d, panel)


def front_kernel(
    ringed, own_plan, plan, place_ref, entry_ref, start_ref, d_ref, agg_ref, trail_ref, *refs
):
    n_own, n_pair = len(own_plan), len(plan)
    own_pieces, pieces = refs[:n_own], refs[n_own : n_own + n_pair]
    out_ref, block_ref = refs[n_own + n_pair : n_own + n_pair + 2]
    own_stage, stage, dt_left, dt_right, own_cat, pair_cat, full, sem = refs[n_own + n_pair + 2 :]
    j, i = pl.program_id(0), pl.program_id(1)
    n_i = pl.num_programs(1)
    bm, bn = out_ref.shape
    width = d_ref.shape[0]
    half = width // 2
    part = width // 4

    def own_copies():
        for n, s in enumerate(own_plan):
            source = ring_place(place_ref[1], s) if ringed else s
            lanes = pl.ds(pl.multiple_of(source * part, part), part)
            yield pltpu.make_async_copy(own_pieces[n], own_stage.at[:, lanes], sem.at[n])

    def pair_copies():
        for n, (upper, steps, swap) in enumerate(plan):
            depth, cols = pieces[n].shape
            block = 0
            if ringed:
                chip = ring_place(place_ref[0] // 2, steps)
                block = (place_ref[0] % 2 ^ swap) * 4 + chip
            at = pl.ds(pl.multiple_of(block * cols, TILE_COLS), cols)
            target = stage.at[pl.ds(upper * depth, depth), at]
            yield pltpu.make_async_copy(pieces[n], target, sem.at[n_own + n])

    @pl.when((i == 0) & (j == 0))
    def _():
        for c in own_copies():
            c.start()
        for c in pair_copies():
            c.start()
        hi, lo = split(d_ref[...].T)
        dt_left[...] = jnp.concatenate(
            [hi[:half, :half], hi[:half, :half], lo[:half, :half]], axis=0
        )
        dt_right[...] = jnp.concatenate([hi[:, half:], hi[:, half:], lo[:, half:]], axis=0)
        for c in own_copies():
            c.wait()

    rows = pl.ds(pl.multiple_of(i * bm, bm), bm)

    @pl.when(j == 0)
    def _():
        hi, lo = split(own_stage[rows, :])
        lhs = jnp.concatenate([hi[:, :half], lo[:, :half], hi[:, :half]], axis=1)
        full[:, :half] = lax.dot_general(
            lhs, dt_left[...], NN, preferred_element_type=jnp.float32
        )
        lhs = jnp.concatenate([hi, lo, hi], axis=1)
        full[:, half:] = lax.dot_general(
            lhs, dt_right[...], NN, preferred_element_type=jnp.float32
        )
        block_ref[...] = full[:, pl.ds(pl.multiple_of(place_ref[1] * part, part), part)]
        hi, lo = split(full[...])
        own_cat[rows, :] = jnp.concatenate([hi, hi, lo], axis=1)

    @pl.when((i == 0) & (j == 0))
    def _():
        for c in pair_copies():
            c.wait()

    @pl.when(i == 0)
    def _():
        cols = pl.ds(pl.multiple_of(j * bn, bn), bn)
        hi, lo = split(stage[:, cols])
        pair_cat[0:width, :] = hi
        pair_cat[width : 2 * width, :] = lo
        pair_cat[2 * width :, :] = hi

    for n in range(0, bn, 256):
        at = slice(n, n + 256)
        product = lax.dot_general(
            own_cat[rows, :], pair_cat[:, at], NN, preferred_element_type=jnp.float32
        )
        out_ref[:, at] = trail_ref[:, at] - product
    step = j * n_i + i

    def add(e, carry):
        r = pl.multiple_of(entry_ref[1, e], TILE_ROWS)
        c = pl.multiple_of(entry_ref[2, e], TILE_COLS)
        here = (pl.ds(r, TILE_ROWS), pl.ds(c, TILE_COLS))
        out_ref[here] = out_ref[here] + agg_ref[entry_ref[0, e]]
        return carry

    lax.fori_loop(start_ref[step], start_ref[step + 1], add, 0)


def front(place, entries, starts, d, agg, trailing, own, own_plan, pieces, plan, ringed, bm, bn):
    rows, cols = trailing.shape
    width = d.shape[0]
    half, part = width // 2, width // 4
    n_i = rows // bm
    whole = pl.BlockSpec(memory_space=pltpu.VMEM)
    smem = pl.BlockSpec(memory_space=pltpu.SMEM)
    block = pl.BlockSpec((bm, bn), lambda j, i: (i, j))
    operands = len(own) + len(pieces)
    return pl.pallas_call(
        functools.partial(front_kernel, ringed, own_plan, plan),
        grid=(cols // bn, n_i),
        out_shape=(
            jax.ShapeDtypeStruct((rows, cols), jnp.float32),
            jax.ShapeDtypeStruct((rows, part), jnp.float32),
        ),
        in_specs=[smem, smem, smem, whole, whole, block]
        + [pl.BlockSpec(memory_space=pl.ANY)] * operands,
        out_specs=(
            block,
            pl.BlockSpec((bm, part), lambda j, i: (jnp.where(j == 0, i, n_i - 1), 0)),
        ),
        scratch_shapes=[
            pltpu.VMEM((rows, width), jnp.float32),
            pltpu.VMEM((width, cols), jnp.float32),
            pltpu.VMEM((3 * half, half), jnp.bfloat16),
            pltpu.VMEM((3 * width, half), jnp.bfloat16),
            pltpu.VMEM((rows, 3 * width), jnp.bfloat16),
            pltpu.VMEM((3 * width, bn), jnp.bfloat16),
            pltpu.VMEM((bm, width), jnp.float32),
            pltpu.SemaphoreType.DMA((operands,)),
        ],
        compiler_params=pltpu.CompilerParams(vmem_limit_bytes=VMEM_LIMIT),
        cost_estimate=pl.CostEstimate(
            flops=6 * rows * width * (cols + width),
            bytes_accessed=8 * rows * cols + 4 * width * cols,
            transcendentals=0,
        ),
        name="front",
    )(place, entries, starts, d, agg, trailing, *own, *pieces)


def pack_tiles(agg_vals, agg_dest, agg_tile, tiles_dev):
    row_devices = lax.axis_size("row")
    agg = agg_vals.shape[2]
    targets = agg_dest.reshape(-1)
    tile_ids = agg_tile.reshape(-1)
    slots = row_devices * CAP
    order = jnp.arange(agg, dtype=jnp.int32)
    earlier = (targets[None, :] == targets[:, None]) & (order[None, :] < order[:, None])
    position = targets * CAP + jnp.sum(earlier.astype(jnp.int32), axis=1)
    hit = position[None, :] == jnp.arange(slots, dtype=jnp.int32)[:, None]
    send_ids = tiles_dev + jnp.sum(jnp.where(hit, tile_ids[None, :] - tiles_dev, 0), axis=1)
    values = agg_vals.reshape(agg, TILE_ROWS, TILE_COLS)
    send = jnp.zeros((slots, TILE_ROWS, TILE_COLS), jnp.float32).at[position].set(values)
    send = send.reshape(row_devices, CAP, TILE_ROWS, TILE_COLS)
    numbers = send_ids.astype(jnp.float32).reshape(row_devices, 1, 1, CAP)
    numbers = jnp.pad(numbers, ((0, 0), (0, 0), (0, TILE_ROWS - 1), (0, TILE_COLS - CAP)))
    return jnp.concatenate([send, numbers], axis=1)


def unpack_tiles(got, tiles_dev):
    landing = got[:, CAP, 0, :CAP].astype(jnp.int32)
    landing = jnp.pad(landing, ((0, 0), (0, 1)), constant_values=tiles_dev)
    return got.reshape(-1, TILE_ROWS, TILE_COLS), landing.reshape(-1)


def order_tiles(landing, slots, tiles_dev, tile_cols, bm, bn, n_i, n_j):
    row = (landing // tile_cols) * TILE_ROWS
    col = (landing % tile_cols) * TILE_COLS
    count = landing.shape[0]
    number = jnp.arange(count, dtype=jnp.int32)
    step = jnp.where(landing < tiles_dev, (col // bn) * n_i + row // bm, n_i * n_j)
    key = step * count + number
    rank = jnp.sum((key[None, :] < key[:, None]).astype(jnp.int32), axis=1)
    hit = (rank[None, :] == jnp.arange(slots, dtype=jnp.int32)[:, None]).astype(jnp.int32)
    fields = jnp.stack([number, row % bm, col % bn])
    entries = jnp.sum(hit[None] * fields[:, None, :], axis=2)
    edges = jnp.arange(n_i * n_j + 1, dtype=jnp.int32)
    starts = jnp.sum((step[None, :] < edges[:, None]).astype(jnp.int32), axis=1)
    return entries, starts


def per_device(diag_inverse, panel, trailing, agg_vals, agg_dest, agg_tile):
    row_devices = lax.axis_size("row")
    col_devices = lax.axis_size("col")
    local_rows, local_cols = trailing.shape
    part = panel.shape[1]
    col_index = lax.axis_index("col")
    tile_cols = local_cols // TILE_COLS
    tiles_dev = (local_rows // TILE_ROWS) * tile_cols
    bm, bn = local_rows, 512
    n_i, n_j = local_rows // bm, local_cols // bn

    row_index = lax.axis_index("row")
    place = jnp.stack([row_index, col_index]).astype(jnp.int32)
    tiles = pack_tiles(agg_vals, agg_dest, agg_tile, tiles_dev)
    tiles = lax.all_to_all(tiles, "row", split_axis=0, concat_axis=0, tiled=True)
    ringed = row_devices == 8 and col_devices == 4
    if ringed:
        quarter = local_rows // 4
        ring = functools.partial(lax.ppermute, axis_name="col", perm=list(NEXT.items()))
        spread = lax.all_to_all(
            panel.reshape(4, quarter, part),
            "row",
            split_axis=0,
            concat_axis=0,
            axis_index_groups=[[0, 2, 4, 6], [1, 3, 5, 7]],
            tiled=True,
        )
        spread, first, tiles = lax.optimization_barrier((spread, ring(panel), tiles))
        wanted = lax.all_to_all(spread, "col", split_axis=0, concat_axis=0, tiled=True)
        wanted, first, mine, tiles = lax.optimization_barrier((wanted, first, panel, tiles))
        third = lax.ppermute(mine, "col", list(PREV.items()))
        second = ring(first)
        siblings = [(p, p ^ 1) for p in range(row_devices)]
        turns = [
            [(2 * c + m, 2 * step[c] + m) for c in range(4) for m in range(2)]
            for step in (NEXT, PREV)
        ]
        held = list(pair_factor(diag_inverse, wanted, quarter))
        pieces, plan = [], []
        for n in range(4):
            if n > 0:
                held = [lax.ppermute(x, "row", turn) for x, turn in zip(held, turns)]
            if n == 1:
                *held, third = lax.optimization_barrier((*held, third))
            for h, x in enumerate(held):
                steps = n if h == 0 else -n
                plan += [(h, steps, 0), (h, steps, 1)]
                pieces += [x, lax.ppermute(x, "row", siblings)]
        own = [panel, first, second, third]
    else:
        whole = lax.all_gather(panel, "col", axis=0)
        column = lax.all_gather(panel, "row", axis=0, tiled=True)
        column = column.reshape(col_devices, local_cols, part)
        partner = lax.all_to_all(column, "col", split_axis=0, concat_axis=0, tiled=True)
        pieces, plan = pair_factor(diag_inverse, partner, 768), [(0, 0, 0), (1, 0, 0)]
        own = [whole[s] for s in range(col_devices)]

    agg, landing = unpack_tiles(tiles, tiles_dev)
    entries, starts = order_tiles(
        landing, row_devices * CAP, tiles_dev, tile_cols, bm, bn, n_i, n_j
    )
    return front(
        place,
        entries,
        starts,
        diag_inverse,
        agg,
        trailing,
        own,
        list(range(4)),
        pieces,
        plan,
        ringed,
        bm,
        bn,
    )


def solution(mesh):
    in_specs = (
        P(),
        P("row", "col"),
        P("row", "col"),
        P("row", "col", None, None),
        P("row", "col", None, None),
        P("row", "col", None),
    )
    out_specs = (P("row", "col"), P("row", "col"))
    return jax.shard_map(
        per_device, mesh=mesh, in_specs=in_specs, out_specs=out_specs, check_vma=False
    )
```

```python
import functools

import jax
import jax.numpy as jnp
from jax import lax
from jax.experimental import pallas as pl
from jax.experimental.pallas import tpu as pltpu
from jax.sharding import PartitionSpec as P

TILE_ROWS = 8
TILE_COLS = 128
CAP = 2
VMEM_LIMIT = 58 << 20
NEXT = {0: 1, 1: 3, 3: 2, 2: 0}
PREV = {v: k for k, v in NEXT.items()}
NN = (((1,), (0,)), ((), ()))
NT = (((1,), (1,)), ((), ()))


def split(x):
    hi = x.astype(jnp.bfloat16)
    lo = (x - hi.astype(jnp.float32)).astype(jnp.bfloat16)
    return hi, lo


def ring_place(index, steps):
    at = (index ^ (index >> 1)) - steps & 3
    return at ^ (at >> 1)


def pair_kernel(d_ref, panel_ref, top_ref, low_ref):
    width = d_ref.shape[0]
    half = width // 2
    d_hi, d_lo = split(d_ref[...])
    hi, lo = split(jnp.concatenate([panel_ref[s] for s in range(4)], axis=1))
    for ref, rows, upto in ((top_ref, slice(0, half), half), (low_ref, slice(half, width), width)):
        d_rows = d_hi[rows, :upto]
        lhs = jnp.concatenate([d_rows, d_rows, d_lo[rows, :upto]], axis=1)
        rhs = jnp.concatenate([hi[:, :upto], lo[:, :upto], hi[:, :upto]], axis=1)
        ref[...] = lax.dot_general(lhs, rhs, NT, preferred_element_type=jnp.float32)


def pair_factor(d, panel, rows_step):
    width = d.shape[0]
    parts, rows, part = panel.shape
    out = jax.ShapeDtypeStruct((width // 2, rows), jnp.float32)
    out_block = pl.BlockSpec((width // 2, rows_step), lambda n: (0, n))
    return pl.pallas_call(
        pair_kernel,
        grid=(rows // rows_step,),
        out_shape=(out, out),
        in_specs=[
            pl.BlockSpec((width, width), lambda n: (0, 0)),
            pl.BlockSpec((parts, rows_step, part), lambda n: (0, n, 0)),
        ],
        out_specs=(out_block, out_block),
        compiler_params=pltpu.CompilerParams(vmem_limit_bytes=VMEM_LIMIT),
        cost_estimate=pl.CostEstimate(
            flops=6 * rows * width * width, bytes_accessed=8 * rows * width, transcendentals=0
        ),
        name="pair_factor",
    )(d, panel)


def front_kernel(
    ringed, own_plan, plan, place_ref, entry_ref, start_ref, d_ref, agg_ref, trail_ref, *refs
):
    n_own, n_pair = len(own_plan), len(plan)
    own_pieces, pieces = refs[:n_own], refs[n_own : n_own + n_pair]
    out_ref, block_ref = refs[n_own + n_pair : n_own + n_pair + 2]
    own_stage, stage, dt_left, dt_right, own_cat, pair_cat, full, sem = refs[n_own + n_pair + 2 :]
    j, i = pl.program_id(0), pl.program_id(1)
    n_i = pl.num_programs(1)
    bm, bn = out_ref.shape
    width = d_ref.shape[0]
    half = width // 2
    part = width // 4

    def own_copies():
        for n, s in enumerate(own_plan):
            source = ring_place(place_ref[1], s) if ringed else s
            lanes = pl.ds(pl.multiple_of(source * part, part), part)
            yield pltpu.make_async_copy(own_pieces[n], own_stage.at[:, lanes], sem.at[n])

    def pair_copies():
        for n, (upper, steps, swap) in enumerate(plan):
            depth, cols = pieces[n].shape
            block = 0
            if ringed:
                chip = ring_place(place_ref[0] // 2, steps)
                block = (place_ref[0] % 2 ^ swap) * 4 + chip
            at = pl.ds(pl.multiple_of(block * cols, TILE_COLS), cols)
            target = stage.at[pl.ds(upper * depth, depth), at]
            yield pltpu.make_async_copy(pieces[n], target, sem.at[n_own + n])

    @pl.when((i == 0) & (j == 0))
    def _():
        for c in own_copies():
            c.start()
        for c in pair_copies():
            c.start()
        hi, lo = split(d_ref[...].T)
        dt_left[...] = jnp.concatenate(
            [hi[:half, :half], hi[:half, :half], lo[:half, :half]], axis=0
        )
        dt_right[...] = jnp.concatenate([hi[:, half:], hi[:, half:], lo[:, half:]], axis=0)
        for c in own_copies():
            c.wait()

    rows = pl.ds(pl.multiple_of(i * bm, bm), bm)

    @pl.when(j == 0)
    def _():
        hi, lo = split(own_stage[rows, :])
        lhs = jnp.concatenate([hi[:, :half], lo[:, :half], hi[:, :half]], axis=1)
        full[:, :half] = lax.dot_general(
            lhs, dt_left[...], NN, preferred_element_type=jnp.float32
        )
        lhs = jnp.concatenate([hi, lo, hi], axis=1)
        full[:, half:] = lax.dot_general(
            lhs, dt_right[...], NN, preferred_element_type=jnp.float32
        )
        block_ref[...] = full[:, pl.ds(pl.multiple_of(place_ref[1] * part, part), part)]
        hi, lo = split(full[...])
        own_cat[rows, :] = jnp.concatenate([hi, hi, lo], axis=1)

    @pl.when((i == 0) & (j == 0))
    def _():
        for c in pair_copies():
            c.wait()

    @pl.when(i == 0)
    def _():
        cols = pl.ds(pl.multiple_of(j * bn, bn), bn)
        hi, lo = split(stage[:, cols])
        pair_cat[0:width, :] = hi
        pair_cat[width : 2 * width, :] = lo
        pair_cat[2 * width :, :] = hi

    for n in range(0, bn, 256):
        at = slice(n, n + 256)
        product = lax.dot_general(
            own_cat[rows, :], pair_cat[:, at], NN, preferred_element_type=jnp.float32
        )
        out_ref[:, at] = trail_ref[:, at] - product
    step = j * n_i + i

    def add(e, carry):
        r = pl.multiple_of(entry_ref[1, e], TILE_ROWS)
        c = pl.multiple_of(entry_ref[2, e], TILE_COLS)
        here = (pl.ds(r, TILE_ROWS), pl.ds(c, TILE_COLS))
        out_ref[here] = out_ref[here] + agg_ref[entry_ref[0, e]]
        return carry

    lax.fori_loop(start_ref[step], start_ref[step + 1], add, 0)


def front(place, entries, starts, d, agg, trailing, own, own_plan, pieces, plan, ringed, bm, bn):
    rows, cols = trailing.shape
    width = d.shape[0]
    half, part = width // 2, width // 4
    n_i = rows // bm
    whole = pl.BlockSpec(memory_space=pltpu.VMEM)
    smem = pl.BlockSpec(memory_space=pltpu.SMEM)
    block = pl.BlockSpec((bm, bn), lambda j, i: (i, j))
    operands = len(own) + len(pieces)
    return pl.pallas_call(
        functools.partial(front_kernel, ringed, own_plan, plan),
        grid=(cols // bn, n_i),
        out_shape=(
            jax.ShapeDtypeStruct((rows, cols), jnp.float32),
            jax.ShapeDtypeStruct((rows, part), jnp.float32),
        ),
        in_specs=[smem, smem, smem, whole, whole, block]
        + [pl.BlockSpec(memory_space=pl.ANY)] * operands,
        out_specs=(
            block,
            pl.BlockSpec((bm, part), lambda j, i: (jnp.where(j == 0, i, n_i - 1), 0)),
        ),
        scratch_shapes=[
            pltpu.VMEM((rows, width), jnp.float32),
            pltpu.VMEM((width, cols), jnp.float32),
            pltpu.VMEM((3 * half, half), jnp.bfloat16),
            pltpu.VMEM((3 * width, half), jnp.bfloat16),
            pltpu.VMEM((rows, 3 * width), jnp.bfloat16),
            pltpu.VMEM((3 * width, bn), jnp.bfloat16),
            pltpu.VMEM((bm, width), jnp.float32),
            pltpu.SemaphoreType.DMA((operands,)),
        ],
        compiler_params=pltpu.CompilerParams(vmem_limit_bytes=VMEM_LIMIT),
        cost_estimate=pl.CostEstimate(
            flops=6 * rows * width * (cols + width),
            bytes_accessed=8 * rows * cols + 4 * width * cols,
            transcendentals=0,
        ),
        name="front",
    )(place, entries, starts, d, agg, trailing, *own, *pieces)


def pack_tiles(agg_vals, agg_dest, agg_tile, tiles_dev):
    row_devices = lax.axis_size("row")
    agg = agg_vals.shape[2]
    targets = agg_dest.reshape(-1)
    tile_ids = agg_tile.reshape(-1)
    slots = row_devices * CAP
    order = jnp.arange(agg, dtype=jnp.int32)
    earlier = (targets[None, :] == targets[:, None]) & (order[None, :] < order[:, None])
    position = targets * CAP + jnp.sum(earlier.astype(jnp.int32), axis=1)
    hit = position[None, :] == jnp.arange(slots, dtype=jnp.int32)[:, None]
    send_ids = tiles_dev + jnp.sum(jnp.where(hit, tile_ids[None, :] - tiles_dev, 0), axis=1)
    values = agg_vals.reshape(agg, TILE_ROWS, TILE_COLS)
    send = jnp.zeros((slots, TILE_ROWS, TILE_COLS), jnp.float32).at[position].set(values)
    send = send.reshape(row_devices, CAP, TILE_ROWS, TILE_COLS)
    numbers = send_ids.astype(jnp.float32).reshape(row_devices, 1, 1, CAP)
    numbers = jnp.pad(numbers, ((0, 0), (0, 0), (0, TILE_ROWS - 1), (0, TILE_COLS - CAP)))
    return jnp.concatenate([send, numbers], axis=1)


def exchange_tiles(send, tiles_dev):
    got = lax.all_to_all(send, "row", split_axis=0, concat_axis=0, tiled=True)
    landing = got[:, CAP, 0, :CAP].astype(jnp.int32)
    landing = jnp.pad(landing, ((0, 0), (0, 1)), constant_values=tiles_dev)
    return got.reshape(-1, TILE_ROWS, TILE_COLS), landing.reshape(-1)


def order_tiles(landing, slots, tiles_dev, tile_cols, bm, bn, n_i, n_j):
    row = (landing // tile_cols) * TILE_ROWS
    col = (landing % tile_cols) * TILE_COLS
    count = landing.shape[0]
    number = jnp.arange(count, dtype=jnp.int32)
    step = jnp.where(landing < tiles_dev, (col // bn) * n_i + row // bm, n_i * n_j)
    key = step * count + number
    rank = jnp.sum((key[None, :] < key[:, None]).astype(jnp.int32), axis=1)
    hit = (rank[None, :] == jnp.arange(slots, dtype=jnp.int32)[:, None]).astype(jnp.int32)
    fields = jnp.stack([number, row % bm, col % bn])
    entries = jnp.sum(hit[None] * fields[:, None, :], axis=2)
    edges = jnp.arange(n_i * n_j + 1, dtype=jnp.int32)
    starts = jnp.sum((step[None, :] < edges[:, None]).astype(jnp.int32), axis=1)
    return entries, starts


def per_device(diag_inverse, panel, trailing, agg_vals, agg_dest, agg_tile):
    row_devices = lax.axis_size("row")
    col_devices = lax.axis_size("col")
    local_rows, local_cols = trailing.shape
    part = panel.shape[1]
    col_index = lax.axis_index("col")
    tile_cols = local_cols // TILE_COLS
    tiles_dev = (local_rows // TILE_ROWS) * tile_cols
    bm, bn = local_rows, 768
    n_i, n_j = local_rows // bm, local_cols // bn

    row_index = lax.axis_index("row")
    place = jnp.stack([row_index, col_index]).astype(jnp.int32)
    tiles = pack_tiles(agg_vals, agg_dest, agg_tile, tiles_dev)
    ringed = row_devices == 8 and col_devices == 4
    if ringed:
        quarter = local_rows // 4
        ring = functools.partial(lax.ppermute, axis_name="col", perm=list(NEXT.items()))
        spread = lax.all_to_all(
            panel.reshape(4, quarter, part),
            "row",
            split_axis=0,
            concat_axis=0,
            axis_index_groups=[[0, 2, 4, 6], [1, 3, 5, 7]],
            tiled=True,
        )
        spread, first, tiles = lax.optimization_barrier((spread, ring(panel), tiles))
        wanted = lax.all_to_all(spread, "col", split_axis=0, concat_axis=0, tiled=True)
        wanted, first, mine, tiles = lax.optimization_barrier((wanted, first, panel, tiles))
        third = lax.ppermute(mine, "col", list(PREV.items()))
        second = ring(first)
        siblings = [(p, p ^ 1) for p in range(row_devices)]
        turns = [
            [(2 * c + m, 2 * step[c] + m) for c in range(4) for m in range(2)]
            for step in (NEXT, PREV)
        ]
        held = list(pair_factor(diag_inverse, wanted, quarter))
        pieces, plan = [], []
        for n in range(4):
            if n > 0:
                held = [lax.ppermute(x, "row", turn) for x, turn in zip(held, turns)]
            if n == 1:
                *held, third = lax.optimization_barrier((*held, third))
            for h, x in enumerate(held):
                steps = n if h == 0 else -n
                plan += [(h, steps, 0), (h, steps, 1)]
                pieces += [x, lax.ppermute(x, "row", siblings)]
        own = [panel, first, second, third]
    else:
        whole = lax.all_gather(panel, "col", axis=0)
        column = lax.all_gather(panel, "row", axis=0, tiled=True)
        column = column.reshape(col_devices, local_cols, part)
        partner = lax.all_to_all(column, "col", split_axis=0, concat_axis=0, tiled=True)
        pieces, plan = pair_factor(diag_inverse, partner, 768), [(0, 0, 0), (1, 0, 0)]
        own = [whole[s] for s in range(col_devices)]

    agg, landing = exchange_tiles(tiles, tiles_dev)
    entries, starts = order_tiles(
        landing, row_devices * CAP, tiles_dev, tile_cols, bm, bn, n_i, n_j
    )
    return front(
        place,
        entries,
        starts,
        diag_inverse,
        agg,
        trailing,
        own,
        list(range(4)),
        pieces,
        plan,
        ringed,
        bm,
        bn,
    )


def solution(mesh):
    in_specs = (
        P(),
        P("row", "col"),
        P("row", "col"),
        P("row", "col", None, None),
        P("row", "col", None, None),
        P("row", "col", None),
    )
    out_specs = (P("row", "col"), P("row", "col"))
    return jax.shard_map(
        per_device, mesh=mesh, in_specs=in_specs, out_specs=out_specs, check_vma=False
    )
```
